32 devices in a mesh: expert: 16 (over z, y, x), shard: 2 (over core).
Axes of the slice: x: 2, y: 2, z: 4, core: 2. Of those that a mesh axis runs over, the one named last changes fastest.
Arguments:
- tokens: bfloat16 [4096, 768], P('expert'), may hold values from -6 to 6
- attn_gain: float32 [768], replicated, may hold values from 0.25 to 1.75
- query_weight: bfloat16 [768, 768], P(None, 'shard'), may hold values from -0.21875 to 0.21875
- key_weight: bfloat16 [768, 768], P(None, 'shard'), may hold values from -0.21875 to 0.21875
- value_weight: bfloat16 [768, 768], P(None, 'shard'), may hold values from -0.21875 to 0.21875
- output_weight: bfloat16 [768, 768], P('shard'), may hold values from -1.25 to 1.25
- bias_table: float32 [32, 12], P(None, 'shard'), may hold values from -5 to 5
- ffn_gain: float32 [768], replicated, may hold values from 0.25 to 1.75
- router_weight: bfloat16 [768, 16], replicated, may hold values from -0.15625 to 0.15625
- expert_in: bfloat16 [16, 768, 3072], P('expert', None, 'shard'), may hold values from -0.21875 to 0.21875
- expert_out: bfloat16 [16, 3072, 768], P('expert', 'shard'), may hold values from -3.5 to 3.5
- routes: int32 [4096, 1], P(('expert', 'shard')), may hold values from 0 to 15; in each aligned block of 128 rows (0 to 127, 128 to 255, ...) at most 16 rows name the same one
- lengths: int32 [16, 4], P('expert'), may hold values from 1 to 128, as said below
- cotangent: bfloat16 [4096, 768], P(('expert', 'shard')), may hold values from -6 to 6
Outputs:
- block_out: bfloat16 [4096, 768], P(('expert', 'shard'))
- grad_tokens: float32 [4096, 768], P('expert')
- grad_attn_gain: float32 [768], replicated
- grad_query: float32 [768, 768], P(None, 'shard')
- grad_key: float32 [768, 768], P(None, 'shard')
- grad_value: float32 [768, 768], P(None, 'shard')
- grad_output: float32 [768, 768], P('shard')
- grad_table: float32 [32, 12], P(None, 'shard')
- grad_ffn_gain: float32 [768], replicated
- grad_router: float32 [768, 16], replicated
- grad_expert_in: float32 [16, 768, 3072], P('expert', None, 'shard')
- grad_expert_out: float32 [16, 3072, 768], P('expert', 'shard')
The draws below stay inside these ranges and needn't reach their ends.
Inputs may be any that keep to these rules, and one draw needn't show every extreme that they name: Each row gives the lengths of the 4 sequences of one token group in order; they sum to 256, and one of them is exactly 128 long. `routes`: within the 128 rows of one device (aligned blocks), no expert is named by more than 16 rows.
All inputs are finite; a program needn't handle non-finite values.
Results may differ from the reference program's by a relative error of at most 0.017.
Values may be sent and summed in bfloat16 or wider, within the bound.
No kernel may reach another device: no remote copies, remote signals or barrier semaphores. Data moves between devices by JAX's collectives and lax.ppermute only.
A program may use at most 128 MiB of HBM per device.

```python
import math
import jax
import jax.numpy as jnp
import numpy as np
from jax import lax

D = 768
H = 12
HD = 64
FF = 3072
NB = 32
TOK_DEV = 128
EXPERTS = 16
GROUPS = 16
TOKENS = 4096
CAP = 16
N_EXPERT = 16
N_SHARD = 2


def draw_lengths(key, part):
    key = jax.random.fold_in(key, 11)
    cut_key, place_key = jax.random.split(key)
    row_keys = jax.random.split(cut_key, GROUPS)
    orders = jax.vmap(lambda row_key: jax.random.permutation(row_key, TOK_DEV - 1))(row_keys)
    cut_one = orders[:, 0] + 1
    cut_two = orders[:, 1] + 1
    lower = jnp.minimum(cut_one, cut_two)
    upper = jnp.maximum(cut_one, cut_two)
    first = lower
    second = upper - lower
    third = TOK_DEV - upper
    longest = jnp.full((GROUPS,), TOK_DEV, jnp.int32)
    position = jax.random.randint(place_key, (GROUPS,), 1, 3)
    slot_one = jnp.where(position == 1, longest, second)
    slot_two = jnp.where(position == 1, second, longest)
    return jnp.stack([first, slot_one, slot_two, third], axis=1).astype(jnp.int32)


def levels(own_key, dims, shards, low, top_value):
    def one(axis_at, blocks):
        steps = jax.random.uniform(jax.random.fold_in(jax.random.fold_in(own_key, 6), axis_at), (blocks,), jnp.float32, low / len(shards), top_value / len(shards))
        return jnp.repeat(jnp.exp(steps), dims[axis_at] // blocks).reshape((-1,) + (1,) * (len(dims) - axis_at - 1))

    level = one(*shards[0])
    for cut in shards[1:]:
        level = level * one(*cut)
    return level


def assign_block(stream_key, own, number, rows, number_of, top, reach, skew):
    sequence = jax.random.permutation(stream_key, number_of)
    heavy_load, common = shares(number_of, rows * top, reach, skew, True), shares(number_of, rows * top, reach, skew, False)
    places = jnp.arange(number_of)

    def named(sizes, offset_by):
        used = int((sizes > 0).sum())
        fixed = max(1, used // 4)
        shifted = fixed + (places - fixed + offset_by * (used - fixed)) % max(1, number_of - fixed)
        return jnp.zeros((number_of,), jnp.int32).at[sequence[jnp.where(places < fixed, places, shifted)]].set(jnp.asarray(sizes, jnp.int32))

    sizes = jnp.where(number % 4 == 0, named(heavy_load, number // 4), named(common, number - number // 4 - 1))
    mixed = jax.random.permutation(jax.random.fold_in(own, 3), number_of)
    source_of, sink = mixed[0:number_of // 2 * 2:2], mixed[1:number_of // 2 * 2:2]
    margin = jnp.minimum(sizes[source_of] - 1, reach - sizes[sink]) // 2
    margin = jnp.where((source_of == sequence[0]) | (sink == sequence[0]) | (sizes[sink] == 0), 0, jnp.maximum(margin, 0))
    shifted = jax.random.randint(jax.random.fold_in(own, 4), (number_of // 2,), 0, 1 << 20) % (margin + 1)
    sizes = sizes.at[source_of].add(-shifted).at[sink].add(shifted)
    items = jnp.searchsorted(jnp.cumsum(sizes), jnp.arange(rows * top), side="right").astype(jnp.int32)
    table = items.reshape(top, rows).T
    table = table[jax.random.permutation(jax.random.fold_in(own, 1), rows)]
    offset_by = jax.random.randint(jax.random.fold_in(own, 2), (rows, 1), 0, top)
    return jnp.take_along_axis(table, (jnp.arange(top)[None, :] + offset_by) % top, axis=1)


def shares(amount, total, bound, lean, full):
    weights = [(1 << 20) // math.isqrt(standing ** lean) + 1 for standing in range(1, amount + 1)]
    largest = bound if full else min(bound, max(-(-total // amount), total * weights[0] // sum(weights)))
    least = 1 if total - largest >= amount - 1 else 0
    given, rest = [largest] + [least] * (amount - 1), total - largest - least * (amount - 1)
    while rest > 0:
        free = [i for i in range(1, amount) if given[i] < largest] or [i for i in range(1, amount) if given[i] < bound]
        pool, remaining = sum([weights[i] for i in free]), rest
        for i in free:
            addition = min(bound - given[i], max(1, remaining * weights[i] // pool), rest)
            given[i] = given[i] + addition
            rest = rest - addition
    return np.array(given)


def scatter_about(own_key, shape, deviation, most, cuts=(), kind=jnp.bfloat16):
    array = deviation * jax.random.normal(own_key, shape, jnp.float32)
    if cuts:
        array = array * levels(own_key, shape, cuts, -0.22, 0.18)
    return jnp.clip(array, -most, most).astype(kind)


def setup_inputs(seed: int = 0) -> dict:
    splits = jax.random.split(jax.random.key(seed), 15)
    tokens = scatter_about(splits[0], (TOKENS, D), 1.0, 6.0, ((0, 16),))
    attn_gain = jnp.clip(1.0 + 0.15 * jax.random.normal(splits[1], (D,), jnp.float32), 0.25, 1.75)
    query_weight = scatter_about(splits[2], (D, H * HD), D ** -0.5, 0.21875, ((1, 2),))
    key_weight = scatter_about(splits[3], (D, H * HD), D ** -0.5, 0.21875, ((1, 2),))
    value_weight = scatter_about(splits[4], (D, H * HD), D ** -0.5, 0.21875, ((1, 2),))
    output_weight = scatter_about(splits[5], (H * HD, D), (H * HD // 32) ** -0.5, 1.25, ((0, 2),))
    bias_table = scatter_about(splits[6], (NB, H), 1.0, 5.0, ((1, 2),), jnp.float32)
    ffn_gain = jnp.clip(1.0 + 0.15 * jax.random.normal(splits[7], (D,), jnp.float32), 0.25, 1.75)
    router_weight = scatter_about(splits[8], (D, EXPERTS), 0.025, 0.15625)
    expert_in = scatter_about(splits[9], (EXPERTS, D, FF), D ** -0.5, 0.21875, ((0, 16), (2, 2)))
    expert_out = scatter_about(splits[10], (EXPERTS, FF, D), (2.0 * EXPERTS * FF ** -0.5), 3.5, ((0, 16), (1, 2)))
    routes_keys = jax.random.split(jax.random.fold_in(splits[11], 1), TOKENS // TOK_DEV)
    routes_turns = jax.random.permutation(jax.random.fold_in(splits[11], 3), TOKENS // TOK_DEV)
    routes = jax.vmap(lambda own, number: assign_block(jax.random.fold_in(splits[11], 2), own, number, TOK_DEV, EXPERTS, 1, CAP, 1))(routes_keys, routes_turns).reshape((TOKENS, 1))
    lengths = draw_lengths(jax.random.fold_in(splits[14], 71), 0)
    cotangent = scatter_about(splits[13], (TOKENS, D), 1.0, 6.0, ((0, 32),))
    return {"tokens": tokens, "attn_gain": attn_gain, "query_weight": query_weight, "key_weight": key_weight, "value_weight": value_weight, "output_weight": output_weight, "bias_table": bias_table, "ffn_gain": ffn_gain, "router_weight": router_weight, "expert_in": expert_in, "expert_out": expert_out, "routes": routes, "lengths": lengths, "cotangent": cotangent}


EPSILON = 1e-06
BORDERS = (12, 16, 23, 32, 46, 64, 91)
HIGHEST = lax.Precision.HIGHEST

@jax.custom_vjp
def low(v):
    return lax.optimization_barrier(v.astype(jnp.bfloat16)).astype(jnp.float32)

@jax.custom_vjp
def low_back(v):
    return v

def low_keep(v):
    return (low(v), None)

def low_pass(kept, grad):
    return (grad,)

def back_keep(v):
    return (v, None)

def back_low(kept, grad):
    return (low(grad),)
low.defvjp(low_keep, low_pass)
low_back.defvjp(back_keep, back_low)

def bucket_of(offsets):
    magnitude = jnp.abs(offsets)
    bucket = jnp.minimum(magnitude, 8)
    for border in BORDERS:
        bucket = bucket + (magnitude >= border).astype(jnp.int32)
    return (bucket + 16 * (offsets > 0).astype(jnp.int32)).astype(jnp.int32)

def rms_normed(rows, gain):
    return rows * lax.rsqrt(lax.optimization_barrier(jnp.mean(rows * rows, axis=-1, keepdims=True)) + EPSILON) * gain

def group_mixed(normed_group, lengths_row, query_weight, key_weight, value_weight, bias_table):
    group_rows = normed_group.shape[0]
    heads = bias_table.shape[1]
    queries = low_back(low(jnp.dot(normed_group, query_weight, precision=HIGHEST))).reshape(group_rows, heads, -1)
    keys = low_back(low(jnp.dot(normed_group, key_weight, precision=HIGHEST))).reshape(group_rows, heads, -1)
    values = low_back(low(jnp.dot(normed_group, value_weight, precision=HIGHEST))).reshape(group_rows, heads, -1)
    scale = queries.shape[2] ** (-0.5)
    logits = low_back(jnp.einsum('qhd,khd->hqk', queries, keys, precision=HIGHEST) * scale)
    positions = jnp.arange(group_rows, dtype=jnp.int32)
    buckets = bucket_of(positions[None, :] - positions[:, None])
    scores = logits + jnp.transpose(bias_table[buckets], (2, 0, 1))
    ends = jnp.cumsum(lengths_row).astype(jnp.int32)
    segment = lax.optimization_barrier(jnp.sum((positions[:, None] >= ends[None, :-1]).astype(jnp.int32), axis=1)).astype(jnp.int32)
    scores = jnp.where((segment[:, None] == segment[None, :])[None], scores, -1e+30)
    probs = jax.nn.softmax(scores, axis=-1)
    mixed = jnp.einsum('hqk,khd->qhd', low(probs), values, precision=HIGHEST)
    return low_back(low(mixed)).reshape(group_rows, -1)

def forward(tokens, attn_gain, query_weight, key_weight, value_weight, output_weight, bias_table, ffn_gain, router_weight, expert_in, expert_out, routes, lengths):
    groups = lengths.shape[0]
    width = tokens.shape[1]
    normed = low(rms_normed(tokens, attn_gain))
    grouped = normed.reshape(groups, -1, width)

    def one_group(pair):
        return group_mixed(pair[0], pair[1], query_weight, key_weight, value_weight, bias_table)
    mixed = lax.map(jax.checkpoint(one_group), (grouped, lengths)).reshape(tokens.shape[0], -1)
    hidden = tokens + low_back(jnp.dot(mixed, output_weight, precision=HIGHEST))
    normed_two = low(rms_normed(hidden, ffn_gain))
    logits = low_back(jnp.dot(normed_two, router_weight, precision=HIGHEST))
    router_probs = jax.nn.softmax(logits, axis=-1)
    expert_count = router_weight.shape[1]
    chosen = routes[:, 0].astype(jnp.int32)
    picked = (chosen[:, None] == jnp.arange(expert_count, dtype=jnp.int32)[None, :]).astype(jnp.int32)
    gate_value = lax.optimization_barrier(jnp.sum(router_probs * picked.astype(jnp.float32), axis=1, keepdims=True))
    slot_count = N_EXPERT * N_SHARD * CAP
    ranks = jnp.cumsum(picked, axis=0).astype(jnp.int32) - picked
    target = chosen * slot_count + lax.optimization_barrier(jnp.sum(ranks * picked, axis=1)).astype(jnp.int32)
    filled = jnp.zeros((expert_count * slot_count, width), jnp.float32).at[target].set(low_back(normed_two))

    def one_expert(triple):
        rows_expert, weight_in, weight_out = triple
        pre_act = low_back(jnp.dot(rows_expert, weight_in, precision=HIGHEST))
        active = low(jax.nn.gelu(pre_act, approximate=False))
        return low_back(low(jnp.dot(active, weight_out, precision=HIGHEST)))
    produced = lax.map(jax.checkpoint(one_expert), (filled.reshape(expert_count, slot_count, width), expert_in, expert_out))
    returned = produced.reshape(expert_count * slot_count, width)[target]
    return hidden + gate_value * returned

def reference(tokens, attn_gain, query_weight, key_weight, value_weight, output_weight, bias_table, ffn_gain, router_weight, expert_in, expert_out, routes, lengths, cotangent):
    floats = tuple((item.astype(jnp.float32) for item in (tokens, attn_gain, query_weight, key_weight, value_weight, output_weight, bias_table, ffn_gain, router_weight, expert_in, expert_out)))

    def closed(*params):
        return forward(*params, routes, lengths)
    result, pullback = jax.vjp(closed, *floats)
    grads = pullback(cotangent.astype(jnp.float32))
    return (result.astype(jnp.bfloat16), grads[0], grads[1], grads[2], grads[3], grads[4], grads[5], grads[6], grads[7], grads[8], grads[9], grads[10])
```

```python
import functools

import jax
import jax.numpy as jnp
from jax import lax
from jax.experimental import pallas as pl
from jax.experimental.pallas import tpu as pltpu
from jax.sharding import PartitionSpec as P

EPSILON = 1e-06
BORDERS = (12, 16, 23, 32, 46, 64, 91)
HIGHEST = lax.Precision.HIGHEST
EXCLUDED = -1e30
PLANE = 4
LINE = 4
LOW = jnp.bfloat16
FULL = jnp.float32
GRANT = 56 * 1024 * 1024


def inverse_rms(rows):
    return lax.rsqrt(jnp.mean(rows * rows, axis=-1, keepdims=True) + EPSILON)


def norm_back(rows, scale_rows, gain, grad_normed):
    scaled = grad_normed * gain
    grad_rows = scale_rows * scaled - rows * scale_rows**3 * jnp.mean(
        scaled * rows, axis=-1, keepdims=True
    )
    grad_gain = jnp.sum(grad_normed * rows * scale_rows, axis=0, keepdims=True)
    return (grad_rows, grad_gain)


def product(left, right, left_dim=1, right_dim=0, precision=None):
    return lax.dot_general(
        left,
        right,
        (((left_dim,), (right_dim,)), ((), ())),
        precision=precision,
        preferred_element_type=FULL,
    )


def wrapped_buckets(bucket_total, columns):
    column = lax.broadcasted_iota(jnp.int32, (bucket_total, columns), 1)
    offset = jnp.where(column < columns // 2, column, column - columns)
    magnitude = jnp.abs(offset)
    bucket = jnp.minimum(magnitude, 8)
    for border in BORDERS:
        bucket = bucket + (magnitude >= border).astype(jnp.int32)
    bucket = bucket + 16 * (offset > 0).astype(jnp.int32)
    rows = lax.broadcasted_iota(jnp.int32, (bucket_total, columns), 0)
    return (bucket == rows).astype(FULL)


def run(kernel, outs, operands, scratch=(), scalars=0, after=()):
    count = len(operands)

    def body(*refs):
        kernel(*refs[:count], *refs[count + len(after) :])

    def whole(shape):
        return pl.BlockSpec(shape, lambda: (0,) * len(shape))

    in_specs = [pl.BlockSpec(memory_space=pltpu.SMEM)] * scalars
    in_specs += [whole(item.shape) for item in operands[scalars:]]
    in_specs += [pl.BlockSpec(memory_space=pl.ANY)] * len(after)
    return pl.pallas_call(
        body,
        out_shape=[jax.ShapeDtypeStruct(shape, dtype) for shape, dtype in outs],
        in_specs=in_specs,
        out_specs=[whole(shape) for shape, _ in outs],
        scratch_shapes=list(scratch),
        compiler_params=pltpu.CompilerParams(vmem_limit_bytes=GRANT),
        cost_estimate=pl.CostEstimate(flops=0, bytes_accessed=0, transcendentals=0),
    )(*operands, *after)


def plan_kernel(routes_ref, cotangent_ref, place_ref, sent_ref, *, experts, capacity):
    own_rows, slots = place_ref.shape
    chosen = routes_ref[...]
    picked = chosen == lax.broadcasted_iota(jnp.int32, (own_rows, experts), 1)
    picked_float = picked.astype(FULL)
    earlier = lax.broadcasted_iota(jnp.int32, (own_rows, own_rows), 1) < lax.broadcasted_iota(
        jnp.int32, (own_rows, own_rows), 0
    )
    ranks = product(earlier.astype(FULL).astype(LOW), picked_float.astype(LOW))
    rank = jnp.sum(ranks * picked_float, axis=1, keepdims=True)
    target = chosen * capacity + rank.astype(jnp.int32)
    place = target == lax.broadcasted_iota(jnp.int32, (own_rows, slots), 1)
    place = place.astype(FULL).astype(LOW)
    place_ref[...] = place
    sent_ref[...] = product(place, cotangent_ref[...], 0, 0).astype(LOW)


def forward_kernel(
    lengths_ref,
    tokens_ref,
    gain_ref,
    query_ref,
    key_ref,
    value_ref,
    output_ref,
    table_ref,
    own_ref,
    other_ref,
    qkv_ref,
    probs_ref,
    normed_turned_ref,
    mixed_turned_ref,
    whole_ref,
    turned_ref,
    *,
    head_size,
):
    group_rows = tokens_ref.shape[0]
    own_rows = own_ref.shape[0]
    heads = table_ref.shape[1]
    columns = heads * head_size
    scale = head_size ** (-0.5)
    half = lax.axis_index("shard")
    own_at = pl.multiple_of(half * own_rows, own_rows)
    other_at = pl.multiple_of((1 - half) * own_rows, own_rows)
    inputs = tokens_ref[...].astype(FULL)
    normed = inputs * inverse_rms(inputs) * gain_ref[...]
    whole_ref[...] = normed
    normed_turned_ref[0:own_rows, :] = whole_ref[pl.ds(own_at, own_rows), :].astype(LOW)
    normed_turned_ref[own_rows:, :] = whole_ref[pl.ds(other_at, own_rows), :].astype(LOW)
    normed = normed.astype(LOW)
    queries = product(normed, query_ref[...]).astype(LOW)
    keys = product(normed, key_ref[...]).astype(LOW)
    values = product(normed, value_ref[...]).astype(LOW)
    qkv_ref[:, 0:columns] = queries
    qkv_ref[:, columns : 2 * columns] = keys
    qkv_ref[:, 2 * columns : 3 * columns] = values
    per_offset = product(
        table_ref[...], wrapped_buckets(table_ref.shape[0], group_rows), 0, 0, HIGHEST
    )
    row_at = lax.broadcasted_iota(jnp.int32, (group_rows, group_rows), 0)
    column_at = lax.broadcasted_iota(jnp.int32, (group_rows, group_rows), 1)
    row_part = jnp.zeros((group_rows, group_rows), jnp.int32)
    column_part = jnp.zeros((group_rows, group_rows), jnp.int32)
    end = 0
    for part in range(lengths_ref.shape[1] - 1):
        end = end + lengths_ref[0, part]
        row_part = row_part + (row_at >= end).astype(jnp.int32)
        column_part = column_part + (column_at >= end).astype(jnp.int32)
    same = row_part == column_part
    mixed_parts = []
    for head in range(heads):
        here = slice(head * head_size, (head + 1) * head_size)
        bias = pltpu.roll(
            jnp.broadcast_to(per_offset[head : head + 1, :], (group_rows, group_rows)),
            0,
            1,
            stride=1,
            stride_axis=0,
        )
        scores = product(queries[:, here], keys[:, here], 1, 1)
        scores = jnp.where(same, scores * scale + bias, EXCLUDED)
        raised = jnp.exp(scores - jnp.max(scores, axis=-1, keepdims=True))
        probs = raised * (1.0 / jnp.sum(raised, axis=-1, keepdims=True))
        probs_ref[head] = probs
        mixed_parts.append(product(probs.astype(LOW), values[:, here]))
    mixed = jnp.concatenate(mixed_parts, axis=1)
    turned_ref[...] = mixed
    mixed = mixed.astype(LOW)
    mixed_turned_ref[0:own_rows, :] = turned_ref[pl.ds(own_at, own_rows), :].astype(LOW)
    mixed_turned_ref[own_rows:, :] = turned_ref[pl.ds(other_at, own_rows), :].astype(LOW)
    whole_ref[...] = product(mixed, output_ref[...])
    own_ref[...] = whole_ref[pl.ds(own_at, own_rows), :]
    other_ref[...] = whole_ref[pl.ds(other_at, own_rows), :]


def hidden_kernel(tokens_ref, own_ref, came_ref, gain_ref, place_ref, hidden_ref, sent_ref):
    own_rows = own_ref.shape[0]
    own_at = pl.multiple_of(lax.axis_index("shard") * own_rows, own_rows)
    inputs = tokens_ref[pl.ds(own_at, own_rows), :].astype(FULL)
    hidden = inputs + (own_ref[...] + came_ref[...])
    hidden_ref[...] = hidden
    normed = (hidden * inverse_rms(hidden) * gain_ref[...]).astype(LOW)
    sent_ref[...] = product(place_ref[...], normed, 0, 0).astype(LOW)


def gate_kernel(
    rows_ref,
    grads_ref,
    router_ref,
    normed_ref,
    mixed_ref,
    chances_ref,
    grad_produced_ref,
    normed_own_ref,
    mixed_out_ref,
):
    logits = product(rows_ref[...], router_ref[...])
    raised = jnp.exp(logits - jnp.max(logits, axis=-1, keepdims=True))
    chances = raised * (1.0 / jnp.sum(raised, axis=-1, keepdims=True))
    chosen = lax.broadcasted_iota(jnp.int32, chances.shape, 1) == lax.axis_index("expert")
    gate = jnp.sum(jnp.where(chosen, chances, 0.0), axis=1, keepdims=True)
    chances_ref[...] = chances
    grad_produced_ref[...] = (gate * grads_ref[...].astype(FULL)).astype(LOW)
    normed_own_ref[...] = normed_ref[0 : normed_own_ref.shape[0], :]
    mixed_out_ref[...] = mixed_ref[...]


def expert_kernel(
    rows_ref,
    grad_produced_ref,
    in_own_ref,
    in_came_ref,
    out_own_ref,
    out_came_ref,
    produced_ref,
    grad_rows_ref,
    active_own_ref,
    active_came_ref,
    grad_pre_own_ref,
    grad_pre_came_ref,
    *,
    steps,
):
    step = pl.program_id(0)

    @pl.when(step == 0)
    def _():
        produced_ref[...] = jnp.zeros_like(produced_ref)
        grad_rows_ref[...] = jnp.zeros_like(grad_rows_ref)

    def block(in_ref, out_ref, active_ref, grad_pre_ref):
        pre = product(rows_ref[...], in_ref[...])
        grad_active = product(grad_produced_ref[...], out_ref[...], 1, 1)
        steep = 1.0 / (1.0 + 0.2316419 * jnp.abs(pre))
        density = jnp.exp(-0.5 * pre * pre) * 0.3989422804014327
        tail = 1.330274429
        for factor in (-1.821255978, 1.781477937, -0.356563782, 0.319381530):
            tail = tail * steep + factor
        tail = tail * steep * density
        cumulative = jnp.where(pre >= 0.0, 1.0 - tail, tail)
        active = (pre * cumulative).astype(LOW)
        grad_pre = (grad_active * (cumulative + pre * density)).astype(LOW)
        active_ref[...] = active
        grad_pre_ref[...] = grad_pre
        produced_ref[...] += product(active, out_ref[...])
        grad_rows_ref[...] += product(grad_pre, in_ref[...], 1, 1)

    @pl.when(step < steps // 2)
    def _():
        block(in_own_ref, out_own_ref, active_own_ref, grad_pre_own_ref)

    @pl.when(step >= steps // 2)
    def _():
        block(in_came_ref, out_came_ref, active_came_ref, grad_pre_came_ref)


def finish_kernel(
    produced_ref,
    grad_rows_ref,
    grads_ref,
    chances_ref,
    rows_ref,
    router_ref,
    back_ref,
    grad_back_ref,
    grad_router_ref,
):
    chances = chances_ref[...]
    chosen = lax.broadcasted_iota(jnp.int32, chances.shape, 1) == lax.axis_index("expert")
    gate = jnp.sum(jnp.where(chosen, chances, 0.0), axis=1, keepdims=True)
    produced = produced_ref[...].astype(LOW).astype(FULL)
    back_ref[...] = (gate * produced).astype(LOW)
    grad_gate = jnp.sum(grads_ref[...].astype(FULL) * produced, axis=1, keepdims=True)
    grad_logits = (grad_gate * chances * (chosen.astype(FULL) - gate)).astype(LOW)
    grad_router_ref[...] = product(grad_logits, rows_ref[...], 0, 0)
    grad_back_ref[...] = (
        grad_rows_ref[...] + product(grad_logits, router_ref[...], 1, 1)
    ).astype(LOW)


def apply_expert(rows, grad_produced, in_own, in_came, out_own, out_came):
    slots, width = rows.shape
    units = in_own.shape[1]
    block = 512
    half = units // block
    steps = 2 * half

    def early(step):
        return jnp.minimum(step, half - 1)

    def late(step):
        return jnp.maximum(step - half, 0)

    def fixed(shape):
        return pl.BlockSpec(shape, lambda step: (0, 0))

    def across(rows_here, place):
        return pl.BlockSpec((rows_here, block), lambda step: (0, place(step)))

    def down(place):
        return pl.BlockSpec((block, width), lambda step: (place(step), 0))

    shapes = [
        ((slots, width), FULL),
        ((slots, width), FULL),
    ] + [((slots, units), LOW)] * 4
    return pl.pallas_call(
        functools.partial(expert_kernel, steps=steps),
        grid=(steps,),
        out_shape=[jax.ShapeDtypeStruct(shape, dtype) for shape, dtype in shapes],
        in_specs=[
            fixed((slots, width)),
            fixed((slots, width)),
            across(width, early),
            across(width, late),
            down(early),
            down(late),
        ],
        out_specs=[
            fixed((slots, width)),
            fixed((slots, width)),
            across(slots, early),
            across(slots, late),
            across(slots, early),
            across(slots, late),
        ],
        compiler_params=pltpu.CompilerParams(vmem_limit_bytes=GRANT),
        cost_estimate=pl.CostEstimate(flops=0, bytes_accessed=0, transcendentals=0),
    )(rows, grad_produced, in_own, in_came, out_own, out_came)


def grad_hidden_kernel(
    place_ref,
    returned_ref,
    hidden_ref,
    gain_ref,
    cotangent_ref,
    grad_router_ref,
    attention_ref,
    small_ref,
):
    experts = grad_router_ref.shape[0]
    width = hidden_ref.shape[1]
    hidden = hidden_ref[...]
    grad_normed = product(place_ref[...], returned_ref[...])
    grad_rows, grad_gain = norm_back(hidden, inverse_rms(hidden), gain_ref[...], grad_normed)
    attention_ref[...] = (cotangent_ref[...].astype(FULL) + grad_rows).astype(LOW)
    small_ref[0:experts, :] = grad_router_ref[...]
    small_ref[experts:, :] = jnp.concatenate(
        [grad_gain, jnp.zeros((small_ref.shape[0] - experts - 1, width), FULL)], axis=0
    )


def halves(own_rows):
    half = lax.axis_index("shard")
    own_at = pl.multiple_of(half * own_rows, own_rows)
    other_at = pl.multiple_of((1 - half) * own_rows, own_rows)
    return (own_at, other_at)


def value_back_kernel(
    attention_own_ref,
    attention_came_ref,
    output_ref,
    probs_ref,
    grad_mixed_ref,
    grad_values_ref,
    part_ref,
    part_one_ref,
    part_two_ref,
    part_three_ref,
    attention_ref,
    values_ref,
    turned_ref,
    *,
    head_size,
):
    own_rows = attention_own_ref.shape[0]
    heads = probs_ref.shape[0]
    columns = heads * head_size
    own_at, other_at = halves(own_rows)
    attention_ref[pl.ds(own_at, own_rows), :] = attention_own_ref[...]
    attention_ref[pl.ds(other_at, own_rows), :] = attention_came_ref[...]
    grad_mixed = product(attention_ref[...], output_ref[...], 1, 1).astype(LOW)
    grad_mixed_ref[...] = grad_mixed
    grad_values = []
    for head in range(heads):
        here = slice(head * head_size, (head + 1) * head_size)
        grad_values.append(product(probs_ref[head].astype(LOW), grad_mixed[:, here], 0, 0))
    grad_values = jnp.concatenate(grad_values, axis=1)
    grad_values_ref[...] = grad_values.astype(LOW)
    values_ref[...] = grad_values
    turned_ref[0:columns, 0:own_rows] = values_ref[pl.ds(own_at, own_rows), :].T
    turned_ref[0:columns, own_rows:] = values_ref[pl.ds(other_at, own_rows), :].T
    turned_ref[columns:, 0:own_rows] = attention_own_ref[...].astype(FULL).T
    turned_ref[columns:, own_rows:] = attention_came_ref[...].astype(FULL).T
    mine = lax.rem(lax.axis_index("expert"), PLANE)
    rows = columns // PLANE
    more = attention_own_ref.shape[1] // PLANE
    refs = (part_ref, part_one_ref, part_two_ref, part_three_ref)
    for other, ref in enumerate(refs):
        at = pl.multiple_of((mine ^ other) * rows, 16)
        ref[0:rows, :] = turned_ref[pl.ds(at, rows), :].astype(LOW)
        at = pl.multiple_of((mine ^ other) * more + columns, 16)
        ref[rows:, :] = turned_ref[pl.ds(at, more), :].astype(LOW)


def query_back_kernel(
    grad_mixed_ref,
    grad_values_ref,
    qkv_ref,
    probs_ref,
    query_ref,
    key_ref,
    value_ref,
    back_ref,
    grad_normed_ref,
    grad_table_ref,
    back_out_ref,
    part_ref,
    part_one_ref,
    part_two_ref,
    part_three_ref,
    grads_ref,
    turned_ref,
    *,
    head_size,
    bucket_total,
):
    group_rows = grad_mixed_ref.shape[0]
    own_rows = group_rows // 2
    heads = probs_ref.shape[0]
    columns = heads * head_size
    scale = head_size ** (-0.5)
    own_at, other_at = halves(own_rows)
    back_out_ref[...] = back_ref[...]
    reversal = (
        lax.broadcasted_iota(jnp.int32, (group_rows, group_rows), 0)
        + lax.broadcasted_iota(jnp.int32, (group_rows, group_rows), 1)
        == group_rows - 1
    )
    reversal = reversal.astype(FULL).astype(LOW)
    grad_queries, grad_keys, sums = [], [], []
    for head in range(heads):
        first = head * head_size
        queries = qkv_ref[:, first : first + head_size]
        keys = qkv_ref[:, columns + first : columns + first + head_size]
        values = qkv_ref[:, 2 * columns + first : 2 * columns + first + head_size]
        probs = probs_ref[head]
        grad_probs = product(grad_mixed_ref[:, first : first + head_size], values, 1, 1)
        inner = jnp.sum(probs * grad_probs, axis=-1, keepdims=True)
        grad_scores = probs * (grad_probs - inner)
        upper = grad_scores.astype(LOW)
        rest = (grad_scores - upper.astype(FULL)).astype(LOW)
        backwards = product(reversal, upper) + product(reversal, rest)
        aligned = pltpu.roll(backwards, 1, 1, stride=1, stride_axis=0)
        sums.append(jnp.sum(aligned, axis=0, keepdims=True))
        grad_queries.append(product(upper, keys) * scale)
        grad_keys.append(product(upper, queries, 0, 0) * scale)
    grad_table_ref[...] = product(
        jnp.concatenate(sums, axis=0), wrapped_buckets(bucket_total, group_rows), 1, 1, HIGHEST
    )
    grad_queries = jnp.concatenate(grad_queries, axis=1)
    grad_keys = jnp.concatenate(grad_keys, axis=1)
    grads_ref[:, 0:columns] = grad_queries
    grads_ref[:, columns:] = grad_keys
    turned_ref[:, 0:own_rows] = grads_ref[pl.ds(own_at, own_rows), :].T
    turned_ref[:, own_rows:] = grads_ref[pl.ds(other_at, own_rows), :].T
    mine = lax.rem(lax.axis_index("expert"), PLANE)
    rows = columns // PLANE
    refs = (part_ref, part_one_ref, part_two_ref, part_three_ref)
    for other, ref in enumerate(refs):
        at = pl.multiple_of((mine ^ other) * rows, 16)
        ref[0:rows, :] = turned_ref[pl.ds(at, rows), :].astype(LOW)
        ref[rows:, :] = turned_ref[pl.ds(pl.multiple_of(at + columns, 16), rows), :].astype(LOW)
    grad_normed = product(grad_queries.astype(LOW), query_ref[...], 1, 1)
    grad_normed = grad_normed + product(grad_keys.astype(LOW), key_ref[...], 1, 1)
    grad_normed = grad_normed + product(grad_values_ref[...], value_ref[...], 1, 1)
    grad_normed_ref[...] = grad_normed.astype(LOW)


def grad_tokens_kernel(
    tokens_ref,
    gain_ref,
    normed_own_ref,
    normed_came_ref,
    attention_own_ref,
    attention_came_ref,
    small_own_ref,
    small_came_ref,
    table_ref,
    grad_tokens_ref,
    small_ref,
):
    own_rows = attention_own_ref.shape[0]
    width = tokens_ref.shape[1]
    heads, buckets = table_ref.shape
    half = lax.axis_index("shard")
    own_at = pl.multiple_of(half * own_rows, own_rows)
    other_at = pl.multiple_of((1 - half) * own_rows, own_rows)
    inputs = tokens_ref[...].astype(FULL)
    grad_normed = normed_own_ref[...].astype(FULL) + normed_came_ref[...].astype(FULL)
    grad_rows, grad_gain = norm_back(inputs, inverse_rms(inputs), gain_ref[...], grad_normed)
    grad_tokens_ref[...] = grad_rows
    grad_tokens_ref[pl.ds(own_at, own_rows), :] += attention_own_ref[...].astype(FULL)
    grad_tokens_ref[pl.ds(other_at, own_rows), :] += attention_came_ref[...].astype(FULL)
    summed = small_own_ref[...] + small_came_ref[...]
    table = jnp.concatenate([table_ref[...], jnp.zeros((heads, width - buckets), FULL)], axis=1)
    more = small_ref.shape[0] - summed.shape[0] - heads - 1
    small_ref[...] = jnp.concatenate(
        [summed, grad_gain, table, jnp.zeros((more, width), FULL)], axis=0
    ).astype(small_ref.dtype)


def line_chunks(totals, refs, total_refs):
    mine = lax.rem(lax.axis_index("expert") // PLANE, LINE)
    width = refs[0].shape[1]
    for total, total_ref in zip(totals, total_refs):
        total_ref[...] = total
    for other, ref in enumerate(refs):
        chunks = []
        for total_ref in total_refs:
            rows = total_ref.shape[0] // LINE
            at = pl.multiple_of((mine ^ other) * rows, 8)
            chunk = total_ref[pl.ds(at, rows), :]
            cut = rows * chunk.shape[1] // width
            chunks.append(
                jnp.concatenate(
                    [chunk[start : start + cut] for start in range(0, rows, cut)], axis=1
                )
                if cut != rows
                else chunk
            )
        ref[...] = jnp.concatenate(chunks, axis=0).astype(ref.dtype)


def met(part, normed_near, normed_far):
    own_rows = normed_near.shape[0]
    return product(part[:, 0:own_rows], normed_near) + product(part[:, own_rows:], normed_far)


def first_sums_kernel(*refs):
    parts, nears, fars, mixeds, outs = (refs[4 * at : 4 * at + 4] for at in range(5))
    columns = mixeds[0].shape[1]
    rows = columns // PLANE
    value_total = 0.0
    output_total = 0.0
    for part, near, far, mixed in zip(parts, nears, fars, mixeds):
        value_total = value_total + met(part[0:rows, :], near[...], far[...])
        output_total = output_total + product(part[rows:, :], mixed[...])
    line_chunks((value_total, output_total), outs, refs[20:22])


def second_sums_kernel(*refs):
    parts, nears, fars, outs = (refs[4 * at : 4 * at + 4] for at in range(4))
    total = 0.0
    for part, near, far in zip(parts, nears, fars):
        total = total + met(part[...], near[...], far[...])
    rows = total.shape[0] // 2
    line_chunks((total[0:rows], total[rows:]), outs, refs[16:18])


def line_sum_kernel(first_ref, second_ref, third_ref, fourth_ref, out_ref):
    near = first_ref[...].astype(FULL) + second_ref[...].astype(FULL)
    far = third_ref[...].astype(FULL) + fourth_ref[...].astype(FULL)
    out_ref[...] = (near + far).astype(out_ref.dtype)


def gathered(refs, upper_ref, lower_ref):
    member = lax.rem(lax.axis_index("expert"), PLANE)
    floor = lax.rem(lax.axis_index("expert") // PLANE, LINE)
    owns, rests = refs[0:PLANE], refs[PLANE:]
    chunk_rows = owns[0].shape[0]
    for across in range(PLANE):
        for along in range(LINE):
            if along == 0:
                chunk = owns[across][...]
            else:
                chunk = rests[across][(along - 1) * chunk_rows : along * chunk_rows, :]
            chunk = chunk.astype(FULL)
            first = 0
            for out_ref in (upper_ref, lower_ref):
                rows = out_ref.shape[0] // PLANE // LINE
                at = ((member ^ across) * LINE + (floor ^ along)) * rows
                cut = rows * out_ref.shape[1] // chunk.shape[1]
                for piece in range(rows // cut):
                    place = pl.multiple_of(at + piece * cut, 8)
                    side = slice(piece * out_ref.shape[1], (piece + 1) * out_ref.shape[1])
                    out_ref[pl.ds(place, cut), :] = chunk[first : first + cut, side]
                first = first + cut


def assemble_kernel(*refs):
    upper_ref, lower_ref = refs[2 * PLANE], refs[2 * PLANE + 1]
    gathered(refs[0 : 2 * PLANE], refs[2 * PLANE + 2], refs[2 * PLANE + 3])
    upper_ref[...] = refs[2 * PLANE + 2][...].T
    lower_ref[...] = refs[2 * PLANE + 3][...].T


def shards(
    tokens,
    attn_gain,
    query_weight,
    key_weight,
    value_weight,
    output_weight,
    bias_table,
    ffn_gain,
    router_weight,
    expert_in,
    expert_out,
    routes,
    lengths,
    cotangent,
):
    group_rows, width = tokens.shape
    own_rows = cotangent.shape[0]
    heads = bias_table.shape[1]
    buckets = bias_table.shape[0]
    columns = query_weight.shape[1]
    head_size = columns // heads
    sources = lax.axis_size("expert")
    experts = router_weight.shape[1]
    capacity = 2 * own_rows // experts
    slots = experts * capacity
    beyond = sources // (PLANE * LINE)
    attn_gain = attn_gain.reshape(1, width)
    ffn_gain = ffn_gain.reshape(1, width)

    def swap(item):
        return lax.ppermute(item, "shard", [(0, 1), (1, 0)])

    def hop(item, distance):
        return lax.ppermute(item, "expert", [(at, at ^ distance) for at in range(sources)])

    def around(items, stride):
        return tuple(hop(item, stride * (step + 1)) for step, item in enumerate(items))

    def exchange(rows):
        parts = rows.reshape(sources, capacity * experts // sources, width)
        came = lax.all_to_all(parts, "expert", split_axis=0, concat_axis=0, tiled=True)
        return came.reshape(slots, width)

    def beyond_sum(item):
        if beyond == 1:
            return item
        groups = [
            [near + PLANE * LINE * far for far in range(beyond)] for near in range(PLANE * LINE)
        ]
        return lax.psum(item, "expert", axis_index_groups=groups)

    place, sent_grads = run(
        functools.partial(plan_kernel, experts=experts, capacity=capacity),
        [((own_rows, slots), LOW), ((slots, width), LOW)],
        (routes, cotangent),
    )
    grads = exchange(sent_grads)
    in_own, out_own = expert_in[0], expert_out[0]
    in_came, out_came = swap(in_own), swap(out_own)
    own, other, qkv, probs, normed, mixed = run(
        functools.partial(forward_kernel, head_size=head_size),
        [
            ((own_rows, width), FULL),
            ((own_rows, width), FULL),
            ((group_rows, 3 * columns), LOW),
            ((heads, group_rows, group_rows), FULL),
            ((group_rows, width), LOW),
            ((group_rows, columns), LOW),
        ],
        (
            lengths,
            tokens,
            attn_gain,
            query_weight,
            key_weight,
            value_weight,
            output_weight,
            bias_table,
        ),
        scratch=(pltpu.VMEM((group_rows, width), FULL), pltpu.VMEM((group_rows, columns), FULL)),
        scalars=1,
        after=(place,),
    )
    hidden, sent_rows = run(
        hidden_kernel,
        [((own_rows, width), FULL), ((slots, width), LOW)],
        (tokens, own, swap(other), ffn_gain, place),
        after=(grads, in_came, out_came),
    )
    rows = exchange(sent_rows)
    chances, grad_produced, normed_own, mixed = run(
        gate_kernel,
        [
            ((slots, experts), FULL),
            ((slots, width), LOW),
            ((own_rows, width), LOW),
            ((group_rows, columns), LOW),
        ],
        (rows, grads, router_weight, normed, mixed),
    )
    normed_near = around((normed_own,) * 3, 1)
    mixed_near = around((mixed,) * 3, 1)
    (
        produced,
        grad_rows,
        active_own,
        active_came,
        grad_pre_own,
        grad_pre_came,
    ) = apply_expert(rows, grad_produced, in_own, in_came, out_own, out_came)
    back, grad_back, grad_router = run(
        finish_kernel,
        [((slots, width), LOW), ((slots, width), LOW), ((experts, width), FULL)],
        (produced, grad_rows, grads, chances, rows, router_weight),
        after=normed_near + mixed_near,
    )
    returned_grads = exchange(grad_back)
    grad_in_other = product(rows, grad_pre_came, 0, 0).astype(jnp.bfloat16)
    grad_out_other = product(active_came, grad_produced, 0, 0).astype(jnp.bfloat16)
    small_rows = -(-(experts + 1) // 8) * 8
    attention_own, small_own = run(
        grad_hidden_kernel,
        [((own_rows, width), LOW), ((small_rows, width), FULL)],
        (place, returned_grads, hidden, ffn_gain, cotangent, grad_router),
        after=(grad_in_other, grad_out_other),
    )
    grad_in_came, grad_out_came = swap(grad_in_other), swap(grad_out_other)
    attention_came = swap(attention_own)
    part_rows = columns // PLANE
    grad_mixed, grad_values, *first_parts = run(
        functools.partial(value_back_kernel, head_size=head_size),
        [((group_rows, columns), LOW), ((group_rows, columns), LOW)]
        + [((part_rows + width // PLANE, group_rows), LOW)] * PLANE,
        (attention_own, attention_came, output_weight, probs),
        scratch=(
            pltpu.VMEM((group_rows, width), LOW),
            pltpu.VMEM((group_rows, columns), FULL),
            pltpu.VMEM((columns + width, group_rows), FULL),
        ),
    )
    first_parts = (first_parts[0],) + around(first_parts[1:], 1)
    grad_normed_own, grad_table, back, *second_parts = run(
        functools.partial(query_back_kernel, head_size=head_size, bucket_total=buckets),
        [((group_rows, width), LOW), ((heads, buckets), FULL), ((slots, width), LOW)]
        + [((2 * part_rows, group_rows), LOW)] * PLANE,
        (
            grad_mixed,
            grad_values,
            qkv,
            probs,
            query_weight,
            key_weight,
            value_weight,
            back,
        ),
        scratch=(
            pltpu.VMEM((group_rows, 2 * columns), FULL),
            pltpu.VMEM((2 * columns, group_rows), FULL),
        ),
    )
    second_parts = (second_parts[0],) + around(second_parts[1:], 1)
    grad_normed_came = swap(grad_normed_own)
    small_came = swap(small_own)
    nears = (normed[0:own_rows],) + normed_near
    fars = (normed[own_rows:],) + tuple(swap(item) for item in normed_near)
    line_rows = part_rows // LINE
    first_chunks = run(
        first_sums_kernel,
        [((2 * line_rows, width), LOW)] * LINE,
        first_parts + nears + fars + (mixed,) + mixed_near,
        scratch=(pltpu.VMEM((part_rows, width), FULL), pltpu.VMEM((width // PLANE, columns), FULL)),
    )
    first_chunks = (first_chunks[0],) + around(first_chunks[1:], PLANE)
    grad_tokens, small = run(
        grad_tokens_kernel,
        [
            ((group_rows, width), FULL),
            ((small_rows + -(-(heads + 1) // 8) * 8, width), LOW),
        ],
        (
            tokens,
            attn_gain,
            grad_normed_own,
            grad_normed_came,
            attention_own,
            attention_came,
            small_own,
            small_came,
            grad_table,
        ),
    )
    second_chunks = run(
        second_sums_kernel,
        [((2 * line_rows, width), LOW)] * LINE,
        second_parts + nears + fars,
        scratch=(pltpu.VMEM((part_rows, width), FULL), pltpu.VMEM((part_rows, width), FULL)),
    )
    second_chunks = (second_chunks[0],) + around(second_chunks[1:], PLANE)
    returned = exchange(back)
    block_out = (
        hidden + jnp.dot(place, returned, preferred_element_type=jnp.float32)
    ).astype(jnp.bfloat16)

    def line_sum(chunks, dtype):
        (chunk,) = run(line_sum_kernel, [(chunks[0].shape, dtype)], chunks)
        return chunk

    def gather(chunks):
        chunk = line_sum(chunks, FULL if beyond > 1 else LOW)
        chunk = beyond_sum(chunk).astype(LOW)
        along = jnp.concatenate(around((chunk,) * 3, PLANE), axis=0)
        across = (chunk,) + around((chunk,) * 3, 1)
        return across + (along,) + around((along,) * 3, 1)

    small = (small,) + around((small,) * 3, PLANE)
    small = beyond_sum(line_sum(small, FULL)).astype(LOW)
    small = (small,) + around((small,) * 3, 1)
    small = line_sum(small, FULL)
    first_all = gather(first_chunks)
    second_all = gather(second_chunks)
    grad_expert_in = product(rows, grad_pre_own, 0, 0) + grad_in_came.astype(jnp.float32)
    grad_expert_out = product(active_own, grad_produced, 0, 0) + grad_out_came.astype(jnp.float32)
    grad_value, grad_output = run(
        assemble_kernel,
        [((width, columns), FULL), ((columns, width), FULL)],
        first_all,
        scratch=(pltpu.VMEM((columns, width), FULL), pltpu.VMEM((width, columns), FULL)),
        after=(grad_expert_in, grad_expert_out),
    )
    grad_query, grad_key = run(
        assemble_kernel,
        [((width, columns), FULL)] * 2,
        second_all,
        scratch=(pltpu.VMEM((columns, width), FULL), pltpu.VMEM((columns, width), FULL)),
    )
    grad_router = small[0:experts].T
    grad_ffn_gain = small[experts]
    grad_attn_gain = small[small_rows]
    grad_table = small[small_rows + 1 : small_rows + 1 + heads, 0:buckets].T

    return (
        block_out,
        grad_tokens,
        grad_attn_gain,
        grad_query,
        grad_key,
        grad_value,
        grad_output,
        grad_table,
        grad_ffn_gain,
        grad_router,
        grad_expert_in[None],
        grad_expert_out[None],
    )


def solution(mesh):
    return jax.shard_map(
        shards,
        mesh=mesh,
        in_specs=(
            P("expert", None),
            P(),
            P(None, "shard"),
            P(None, "shard"),
            P(None, "shard"),
            P("shard", None),
            P(None, "shard"),
            P(),
            P(),
            P("expert", None, "shard"),
            P("expert", "shard", None),
            P(("expert", "shard"), None),
            P("expert", None),
            P(("expert", "shard"), None),
        ),
        out_specs=(
            P(("expert", "shard"), None),
            P("expert", None),
            P(),
            P(None, "shard"),
            P(None, "shard"),
            P(None, "shard"),
            P("shard", None),
            P(None, "shard"),
            P(),
            P(),
            P("expert", None, "shard"),
            P("expert", "shard", None),
        ),
        check_vma=False,
    )
```

```python
import functools

import jax
import jax.numpy as jnp
from jax import lax
from jax.experimental import pallas as pl
from jax.experimental.pallas import tpu as pltpu
from jax.sharding import PartitionSpec as P

EPSILON = 1e-06
BORDERS = (12, 16, 23, 32, 46, 64, 91)
HIGHEST = lax.Precision.HIGHEST
EXCLUDED = -1e30
PLANE = 4
LINE = 4
LOW = jnp.bfloat16
FULL = jnp.float32
GRANT = 56 * 1024 * 1024
LITTLE = 4 * 1024 * 1024


def inverse_rms(rows):
    return lax.rsqrt(jnp.mean(rows * rows, axis=-1, keepdims=True) + EPSILON)


def norm_back(rows, scale_rows, gain, grad_normed):
    scaled = grad_normed * gain
    grad_rows = scale_rows * scaled - rows * scale_rows**3 * jnp.mean(
        scaled * rows, axis=-1, keepdims=True
    )
    grad_gain = jnp.sum(grad_normed * rows * scale_rows, axis=0, keepdims=True)
    return (grad_rows, grad_gain)


def product(left, right, left_dim=1, right_dim=0, precision=None):
    return lax.dot_general(
        left,
        right,
        (((left_dim,), (right_dim,)), ((), ())),
        precision=precision,
        preferred_element_type=FULL,
    )


def wrapped_buckets(bucket_total, columns):
    column = lax.broadcasted_iota(jnp.int32, (bucket_total, columns), 1)
    offset = jnp.where(column < columns // 2, column, column - columns)
    magnitude = jnp.abs(offset)
    bucket = jnp.minimum(magnitude, 8)
    for border in BORDERS:
        bucket = bucket + (magnitude >= border).astype(jnp.int32)
    bucket = bucket + 16 * (offset > 0).astype(jnp.int32)
    rows = lax.broadcasted_iota(jnp.int32, (bucket_total, columns), 0)
    return (bucket == rows).astype(FULL)


class Fetched:
    def __init__(self, ref, copy):
        self.ref = ref
        self.copy = copy
        self.shape = ref.shape

    def ready(self):
        if self.copy is not None:
            self.copy.wait()
            self.copy = None

    def __getitem__(self, index):
        self.ready()
        return self.ref[index]


class Sent:
    def __init__(self, ref, copy):
        self.ref = ref
        self.copy = copy
        self.shape = ref.shape
        self.dtype = ref.dtype
        self.started = False

    def __getitem__(self, index):
        return self.ref[index]

    def __setitem__(self, index, value):
        self.ref[index] = value

    def send(self):
        if not self.started:
            self.copy.start()
            self.started = True


def run(kernel, outs, operands, scratch=(), scalars=0, raw=(), after=(), near=False):
    count, results = len(operands), len(outs)
    brought = [] if near else [at for at in range(scalars, count) if at not in raw]

    def body(*refs):
        refs = list(refs)
        given = refs[:count]
        rest = refs[count + len(after) :]
        targets, rest = rest[:results], rest[results:]
        if near:
            kernel(*given, *targets, *rest)
            return
        own, rest = rest[: len(scratch)], rest[len(scratch) :]
        buffers, rest = rest[: len(brought)], rest[len(brought) :]
        built, (arrived, left) = rest[:results], rest[results:]
        for slot, (at, buffer) in enumerate(zip(brought, buffers)):
            copy = pltpu.make_async_copy(given[at], buffer, arrived.at[slot])
            copy.start()
            given[at] = Fetched(buffer, copy)
        sent = [
            Sent(buffer, pltpu.make_async_copy(buffer, target, left.at[slot]))
            for slot, (buffer, target) in enumerate(zip(built, targets))
        ]
        kernel(*given, *sent, *own)
        for at in brought:
            given[at].ready()
        for item in sent:
            item.send()
        for item in sent:
            item.copy.wait()

    anywhere = pl.BlockSpec(memory_space=pl.ANY)
    placed = pl.BlockSpec(memory_space=pltpu.VMEM) if near else anywhere
    in_specs = [pl.BlockSpec(memory_space=pltpu.SMEM)] * scalars
    in_specs += [placed] * (count - scalars) + [anywhere] * len(after)
    scratch_shapes = list(scratch)
    if not near:
        scratch_shapes += [pltpu.VMEM(operands[at].shape, operands[at].dtype) for at in brought]
        scratch_shapes += [pltpu.VMEM(shape, dtype) for shape, dtype in outs]
        scratch_shapes += [pltpu.SemaphoreType.DMA((len(brought),))]
        scratch_shapes += [pltpu.SemaphoreType.DMA((results,))]
    return pl.pallas_call(
        body,
        out_shape=[jax.ShapeDtypeStruct(shape, dtype) for shape, dtype in outs],
        in_specs=in_specs,
        out_specs=[placed] * results,
        scratch_shapes=scratch_shapes,
        compiler_params=pltpu.CompilerParams(vmem_limit_bytes=LITTLE if near else GRANT),
        cost_estimate=pl.CostEstimate(flops=0, bytes_accessed=0, transcendentals=0),
    )(*operands, *after)


def placed_rows(chosen, experts, capacity, slots):
    own_rows = chosen.shape[1]
    picked = chosen == lax.broadcasted_iota(jnp.int32, (experts, own_rows), 0)
    picked_float = picked.astype(FULL)
    earlier = lax.broadcasted_iota(jnp.int32, (own_rows, own_rows), 0) < lax.broadcasted_iota(
        jnp.int32, (own_rows, own_rows), 1
    )
    ranks = product(picked_float.astype(LOW), earlier.astype(FULL).astype(LOW))
    rank = jnp.sum(ranks * picked_float, axis=0, keepdims=True)
    target = chosen * capacity + rank.astype(jnp.int32)
    place = target == lax.broadcasted_iota(jnp.int32, (slots, own_rows), 0)
    return place.astype(FULL).astype(LOW)


def forward_kernel(
    lengths_ref,
    tokens_ref,
    gain_ref,
    query_ref,
    key_ref,
    value_ref,
    table_ref,
    output_ref,
    own_ref,
    other_ref,
    qkv_ref,
    probs_ref,
    normed_turned_ref,
    mixed_ref,
    whole_ref,
    *,
    head_size,
):
    group_rows = tokens_ref.shape[0]
    own_rows = own_ref.shape[0]
    heads, buckets = table_ref.shape
    columns = heads * head_size
    scale = head_size ** (-0.5)
    half = lax.axis_index("shard")
    own_at = pl.multiple_of(half * own_rows, own_rows)
    other_at = pl.multiple_of((1 - half) * own_rows, own_rows)
    inputs = tokens_ref[...].astype(FULL)
    normed = inputs * inverse_rms(inputs) * gain_ref[...].reshape(1, -1)
    whole_ref[...] = normed
    normed_turned_ref[0:own_rows, :] = whole_ref[pl.ds(own_at, own_rows), :].astype(LOW)
    normed_turned_ref[own_rows:, :] = whole_ref[pl.ds(other_at, own_rows), :].astype(LOW)
    normed = normed.astype(LOW)
    queries = product(normed, query_ref[...]).astype(LOW)
    keys = product(normed, key_ref[...]).astype(LOW)
    values = product(normed, value_ref[...]).astype(LOW)
    qkv_ref[:, 0:columns] = queries
    qkv_ref[:, columns : 2 * columns] = keys
    qkv_ref[:, 2 * columns : 3 * columns] = values
    qkv_ref.send()
    normed_turned_ref.send()
    per_offset = product(
        table_ref[...], wrapped_buckets(buckets, group_rows), 1, 0, HIGHEST
    )
    row_at = lax.broadcasted_iota(jnp.int32, (group_rows, group_rows), 0)
    column_at = lax.broadcasted_iota(jnp.int32, (group_rows, group_rows), 1)
    row_part = jnp.zeros((group_rows, group_rows), jnp.int32)
    column_part = jnp.zeros((group_rows, group_rows), jnp.int32)
    end = 0
    for part in range(lengths_ref.shape[1] - 1):
        end = end + lengths_ref[0, part]
        row_part = row_part + (row_at >= end).astype(jnp.int32)
        column_part = column_part + (column_at >= end).astype(jnp.int32)
    same = row_part == column_part
    mixed_parts = []
    for head in range(heads):
        here = slice(head * head_size, (head + 1) * head_size)
        bias = pltpu.roll(
            jnp.broadcast_to(per_offset[head : head + 1, :], (group_rows, group_rows)),
            0,
            1,
            stride=1,
            stride_axis=0,
        )
        scores = product(queries[:, here], keys[:, here], 1, 1)
        scores = jnp.where(same, scores * scale + bias, EXCLUDED)
        raised = jnp.exp(scores - jnp.max(scores, axis=-1, keepdims=True))
        probs = raised * (1.0 / jnp.sum(raised, axis=-1, keepdims=True))
        probs = probs.astype(LOW)
        probs_ref[head] = probs
        mixed_parts.append(product(probs, values[:, here]))
    probs_ref.send()
    mixed = jnp.concatenate(mixed_parts, axis=1).astype(LOW)
    mixed_ref[...] = mixed
    mixed_ref.send()
    whole_ref[...] = product(mixed, output_ref[...])
    own_ref[...] = whole_ref[pl.ds(own_at, own_rows), :]
    other_ref[...] = whole_ref[pl.ds(other_at, own_rows), :]


def hidden_kernel(
    routes_ref,
    cotangent_ref,
    tokens_ref,
    own_ref,
    gain_ref,
    normed_ref,
    came_ref,
    place_ref,
    hidden_ref,
    sent_ref,
    normed_own_ref,
    *,
    experts,
    capacity,
):
    own_rows, width = own_ref.shape
    slots = place_ref.shape[0]
    place = placed_rows(routes_ref[...], experts, capacity, slots)
    place_ref[...] = place
    place_ref.send()
    sent_ref[:, width:] = product(place, cotangent_ref[...]).astype(LOW)
    own_at = pl.multiple_of(lax.axis_index("shard") * own_rows, own_rows)
    inputs = tokens_ref[pl.ds(own_at, own_rows), :].astype(FULL)
    hidden = inputs + (own_ref[...] + came_ref[...])
    normed = (hidden * inverse_rms(hidden) * gain_ref[...].reshape(1, -1)).astype(LOW)
    sent_ref[:, 0:width] = product(place, normed).astype(LOW)
    sent_ref.send()
    hidden_ref[...] = hidden
    normed_own_ref[...] = normed_ref[0:own_rows, :]


def expert_kernel(
    arrived_ref,
    router_ref,
    in_own_ref,
    out_own_ref,
    in_came_ref,
    out_came_ref,
    back_ref,
    grad_back_ref,
    grad_router_ref,
    rows_ref,
    grad_produced_ref,
    active_own_ref,
    active_came_ref,
    grad_pre_own_ref,
    grad_pre_came_ref,
    in_held_ref,
    out_held_ref,
    arrived,
):
    width, units = in_own_ref.shape
    copies = [
        pltpu.make_async_copy(source, target, arrived.at[at])
        for at, (source, target) in enumerate(
            (
                (in_own_ref, in_held_ref.at[0]),
                (out_own_ref, out_held_ref.at[0]),
                (in_came_ref, in_held_ref.at[1]),
                (out_came_ref, out_held_ref.at[1]),
            )
        )
    ]
    for copy in copies:
        copy.start()
    rows = arrived_ref[:, 0:width]
    grads = arrived_ref[:, width:].astype(FULL)
    rows_ref[...] = rows
    rows_ref.send()
    logits = product(rows, router_ref[...], 1, 1)
    raised = jnp.exp(logits - jnp.max(logits, axis=-1, keepdims=True))
    chances = raised * (1.0 / jnp.sum(raised, axis=-1, keepdims=True))
    chosen = lax.broadcasted_iota(jnp.int32, chances.shape, 1) == lax.axis_index("expert")
    gate = jnp.sum(jnp.where(chosen, chances, 0.0), axis=1, keepdims=True)
    grad_produced = (gate * grads).astype(LOW)
    grad_produced_ref[...] = grad_produced
    grad_produced_ref.send()
    produced = 0.0
    grad_rows = 0.0
    block = 512
    for source in range(2):
        copies[2 * source].wait()
        copies[2 * source + 1].wait()
        active_ref = (active_own_ref, active_came_ref)[source]
        grad_pre_ref = (grad_pre_own_ref, grad_pre_came_ref)[source]
        for first in range(0, units, block):
            here = slice(first, first + block)
            in_block = in_held_ref[source, :, here]
            out_block = out_held_ref[source, here, :]
            pre = product(rows, in_block)
            grad_active = product(grad_produced, out_block, 1, 1)
            steep = 1.0 / (1.0 + 0.2316419 * jnp.abs(pre))
            density = jnp.exp(-0.5 * pre * pre) * 0.3989422804014327
            tail = 1.330274429
            for factor in (-1.821255978, 1.781477937, -0.356563782, 0.319381530):
                tail = tail * steep + factor
            tail = tail * steep * density
            cumulative = jnp.where(pre >= 0.0, 1.0 - tail, tail)
            active = (pre * cumulative).astype(LOW)
            grad_pre = (grad_active * (cumulative + pre * density)).astype(LOW)
            active_ref[:, here] = active
            grad_pre_ref[:, here] = grad_pre
            produced = produced + product(active, out_block)
            grad_rows = grad_rows + product(grad_pre, in_block, 1, 1)
        active_ref.send()
        grad_pre_ref.send()
    produced = produced.astype(LOW).astype(FULL)
    grad_gate = jnp.sum(grads * produced, axis=1, keepdims=True)
    grad_logits = (grad_gate * chances * (chosen.astype(FULL) - gate)).astype(LOW)
    grad_back_ref[...] = (grad_rows + product(grad_logits, router_ref[...])).astype(LOW)
    grad_back_ref.send()
    back_ref[...] = (gate * produced).astype(LOW)
    grad_router_ref[...] = product(grad_logits, rows, 0, 0)


def grad_hidden_kernel(
    place_ref,
    returned_ref,
    hidden_ref,
    gain_ref,
    cotangent_ref,
    grad_router_ref,
    attention_ref,
    small_ref,
):
    experts = grad_router_ref.shape[0]
    width = hidden_ref.shape[1]
    hidden = hidden_ref[...]
    grad_normed = product(place_ref[...], returned_ref[...], 0, 0)
    grad_rows, grad_gain = norm_back(hidden, inverse_rms(hidden), gain_ref[...].reshape(1, -1), grad_normed)
    attention_ref[...] = (cotangent_ref[...].astype(FULL) + grad_rows).astype(LOW)
    small_ref[0:experts, :] = grad_router_ref[...]
    small_ref[experts:, :] = jnp.concatenate(
        [grad_gain, jnp.zeros((small_ref.shape[0] - experts - 1, width), FULL)], axis=0
    )


def halves(own_rows):
    half = lax.axis_index("shard")
    own_at = pl.multiple_of(half * own_rows, own_rows)
    other_at = pl.multiple_of((1 - half) * own_rows, own_rows)
    return (own_at, other_at)


def attention_back_kernel(
    attention_own_ref,
    attention_came_ref,
    output_ref,
    mixed_ref,
    qkv_ref,
    probs_ref,
    query_ref,
    key_ref,
    value_ref,
    back_ref,
    grad_normed_ref,
    grad_table_ref,
    back_out_ref,
    part_ref,
    part_one_ref,
    part_two_ref,
    part_three_ref,
    attention_ref,
    grads_ref,
    turned_ref,
    output_grad_ref,
    *,
    head_size,
    bucket_total,
):
    own_rows, width = attention_own_ref.shape
    group_rows = 2 * own_rows
    heads = probs_ref.shape[0]
    columns = heads * head_size
    scale = head_size ** (-0.5)
    own_at, other_at = halves(own_rows)
    attention_ref[pl.ds(own_at, own_rows), :] = attention_own_ref[...]
    attention_ref[pl.ds(other_at, own_rows), :] = attention_came_ref[...]
    grad_mixed = product(attention_ref[...], output_ref[...], 1, 1).astype(LOW)
    output_grad_ref[...] = product(mixed_ref[...], attention_ref[...], 0, 0)
    reversal = (
        lax.broadcasted_iota(jnp.int32, (group_rows, group_rows), 0)
        + lax.broadcasted_iota(jnp.int32, (group_rows, group_rows), 1)
        == group_rows - 1
    )
    reversal = reversal.astype(FULL).astype(LOW)
    grad_queries, grad_keys, grad_values, sums = [], [], [], []
    for head in range(heads):
        first = head * head_size
        queries = qkv_ref[:, first : first + head_size]
        keys = qkv_ref[:, columns + first : columns + first + head_size]
        values = qkv_ref[:, 2 * columns + first : 2 * columns + first + head_size]
        probs = probs_ref[head].astype(FULL)
        grad_head = grad_mixed[:, first : first + head_size]
        grad_probs = product(grad_head, values, 1, 1)
        inner = jnp.sum(probs * grad_probs, axis=-1, keepdims=True)
        grad_scores = probs * (grad_probs - inner)
        upper = grad_scores.astype(LOW)
        rest = (grad_scores - upper.astype(FULL)).astype(LOW)
        backwards = product(reversal, upper) + product(reversal, rest)
        aligned = pltpu.roll(backwards, 1, 1, stride=1, stride_axis=0)
        sums.append(jnp.sum(aligned, axis=0, keepdims=True))
        grad_queries.append(product(upper, keys) * scale)
        grad_keys.append(product(upper, queries, 0, 0) * scale)
        grad_values.append(product(probs_ref[head], grad_head, 0, 0))
    grad_table_ref[...] = product(
        jnp.concatenate(sums, axis=0), wrapped_buckets(bucket_total, group_rows), 1, 1, HIGHEST
    )
    grad_queries = jnp.concatenate(grad_queries, axis=1)
    grad_keys = jnp.concatenate(grad_keys, axis=1)
    grad_values = jnp.concatenate(grad_values, axis=1)
    grads_ref[:, 0:columns] = grad_values
    grads_ref[:, columns : 2 * columns] = grad_queries
    grads_ref[:, 2 * columns : 3 * columns] = grad_keys
    turned_ref[:, 0:own_rows] = grads_ref[pl.ds(own_at, own_rows), :].T
    turned_ref[:, own_rows:] = grads_ref[pl.ds(other_at, own_rows), :].T
    mine = lax.rem(lax.axis_index("expert"), PLANE)
    rows = columns // PLANE
    refs = (part_ref, part_one_ref, part_two_ref, part_three_ref)
    for other, ref in enumerate(refs):
        for weight in range(3):
            at = pl.multiple_of((mine ^ other) * rows + weight * columns, 16)
            ref[weight * rows : (weight + 1) * rows, :] = turned_ref[pl.ds(at, rows), :].astype(
                LOW
            )
        at = pl.multiple_of((mine ^ other) * rows, 16)
        quarter = output_grad_ref[pl.ds(at, rows), :].astype(LOW)
        for piece in range(width // group_rows):
            ref[(3 + piece) * rows : (4 + piece) * rows, :] = quarter[
                :, piece * group_rows : (piece + 1) * group_rows
            ]
        ref.send()
    back_out_ref[...] = back_ref[...]
    back_out_ref.send()
    grad_normed = product(grad_queries.astype(LOW), query_ref[...], 1, 1)
    grad_normed = grad_normed + product(grad_keys.astype(LOW), key_ref[...], 1, 1)
    grad_normed = grad_normed + product(grad_values.astype(LOW), value_ref[...], 1, 1)
    grad_normed_ref[...] = grad_normed.astype(LOW)


def grad_tokens_kernel(
    tokens_ref,
    gain_ref,
    normed_own_ref,
    normed_came_ref,
    attention_own_ref,
    attention_came_ref,
    small_own_ref,
    small_came_ref,
    table_ref,
    grad_tokens_ref,
    small_ref,
):
    own_rows = attention_own_ref.shape[0]
    width = tokens_ref.shape[1]
    heads, buckets = table_ref.shape
    half = lax.axis_index("shard")
    own_at = pl.multiple_of(half * own_rows, own_rows)
    other_at = pl.multiple_of((1 - half) * own_rows, own_rows)
    inputs = tokens_ref[...].astype(FULL)
    grad_normed = normed_own_ref[...].astype(FULL) + normed_came_ref[...].astype(FULL)
    grad_rows, grad_gain = norm_back(inputs, inverse_rms(inputs), gain_ref[...].reshape(1, -1), grad_normed)
    grad_tokens_ref[...] = grad_rows
    grad_tokens_ref[pl.ds(own_at, own_rows), :] += attention_own_ref[...].astype(FULL)
    grad_tokens_ref[pl.ds(other_at, own_rows), :] += attention_came_ref[...].astype(FULL)
    summed = small_own_ref[...] + small_came_ref[...]
    table = jnp.concatenate([table_ref[...], jnp.zeros((heads, width - buckets), FULL)], axis=1)
    more = small_ref.shape[0] - summed.shape[0] - heads - 1
    small_ref[...] = jnp.concatenate(
        [summed, grad_gain, table, jnp.zeros((more, width), FULL)], axis=0
    ).astype(small_ref.dtype)


def line_chunks(totals, refs, total_refs, shared=()):
    mine = lax.rem(lax.axis_index("expert") // PLANE, LINE)
    for total, total_ref in zip(totals, total_refs):
        total_ref[...] = total
    for other, ref in enumerate(refs):
        chunks = []
        for total_ref in total_refs:
            rows = total_ref.shape[0] // LINE
            at = pl.multiple_of((mine ^ other) * rows, 8)
            chunks.append(total_ref[pl.ds(at, rows), :])
        ref[...] = jnp.concatenate(chunks + list(shared), axis=0).astype(ref.dtype)
        ref.send()


def sums_kernel(*refs):
    parts, nears, fars, normed_ref, small_ref = refs[0:4], refs[4:7], refs[7:10], *refs[10:12]
    outs, total_refs = refs[12:16], refs[16:20]
    own_rows = normed_ref.shape[0] // 2
    rows = total_refs[0].shape[0]
    pieces = normed_ref.shape[1] // parts[0].shape[1]
    output = 0.0
    weights = 0.0
    for at, part in enumerate(parts):
        output = output + jnp.concatenate(
            [part[(3 + piece) * rows : (4 + piece) * rows, :] for piece in range(pieces)], axis=1
        ).astype(FULL)
        near = nears[at - 1][...] if at else normed_ref[0:own_rows]
        far = fars[at - 1][...] if at else normed_ref[own_rows:]
        weights = weights + product(part[0 : 3 * rows, 0:own_rows], near)
        weights = weights + product(part[0 : 3 * rows, own_rows:], far)
    totals = (weights[0:rows], weights[rows : 2 * rows], weights[2 * rows :], output)
    line_chunks(totals, outs, total_refs, (small_ref[...].astype(FULL),))


def summed(refs, rows=slice(None)):
    near = refs[0][rows, :].astype(FULL) + refs[1][rows, :].astype(FULL)
    far = refs[2][rows, :].astype(FULL) + refs[3][rows, :].astype(FULL)
    return near + far


def line_sum_kernel(*refs):
    total = summed(refs[0:LINE])
    for out_ref in refs[LINE:]:
        out_ref[...] = total[0 : out_ref.shape[0]].astype(out_ref.dtype)


def assemble_kernel(*refs):
    chunk_refs = refs[0 : PLANE * LINE]
    value_ref, query_ref, key_ref, output_ref, router_ref, ffn_ref, attn_ref, table_ref = refs[
        PLANE * LINE : -3
    ]
    totals = refs[-3:] + (output_ref.ref,)
    member = lax.rem(lax.axis_index("expert"), PLANE)
    floor = lax.rem(lax.axis_index("expert") // PLANE, LINE)
    rows = output_ref.shape[0] // PLANE // LINE
    for along in range(LINE):
        for across in range(PLANE):
            chunk = chunk_refs[along * PLANE + across][0 : 4 * rows, :].astype(FULL)
            at = pl.multiple_of(((member ^ across) * LINE + (floor ^ along)) * rows, 8)
            for weight, total_ref in enumerate(totals):
                total_ref[pl.ds(at, rows), :] = chunk[weight * rows : (weight + 1) * rows]
    output_ref.send()
    for total_ref, ref in zip(totals, (value_ref, query_ref, key_ref)):
        ref[...] = total_ref[...].T
        ref.send()
    small = summed(chunk_refs[0:PLANE], slice(4 * rows, None))
    experts = router_ref.shape[0]
    heads, buckets = table_ref.shape
    late = -(-(experts + 1) // 8) * 8
    router_ref[...] = small[0:experts]
    ffn_ref[...] = small[experts : experts + 1].reshape(-1)
    attn_ref[...] = small[late : late + 1].reshape(-1)
    table_ref[...] = small[late + 1 : late + 1 + heads, 0:buckets]


def expert_grads_kernel(
    rows_ref,
    rows_far_ref,
    grad_produced_ref,
    grad_produced_far_ref,
    active_ref,
    active_far_ref,
    grad_pre_ref,
    grad_pre_far_ref,
    grad_in_ref,
    grad_out_ref,
    done_ref,
):
    done_ref[...] = jnp.zeros_like(done_ref)
    grad_in_ref[...] = product(rows_ref[...], grad_pre_ref[...], 0, 0) + product(
        rows_far_ref[...], grad_pre_far_ref[...], 0, 0
    )
    grad_out_ref[...] = product(active_ref[...], grad_produced_ref[...], 0, 0) + product(
        active_far_ref[...], grad_produced_far_ref[...], 0, 0
    )


def expert_grads(rows, rows_far, grad_produced, grad_produced_far, *wide):
    slots, width = rows.shape
    units = wide[0].shape[1]
    block = 768
    fixed = pl.BlockSpec((slots, width), lambda step: (0, 0))
    moving = pl.BlockSpec((slots, block), lambda step: (0, step))
    return pl.pallas_call(
        expert_grads_kernel,
        grid=(units // block,),
        out_shape=[
            jax.ShapeDtypeStruct((width, units), FULL),
            jax.ShapeDtypeStruct((units, width), FULL),
            jax.ShapeDtypeStruct((8, 128), FULL),
        ],
        in_specs=[fixed] * 4 + [moving] * 4,
        out_specs=[
            pl.BlockSpec((width, block), lambda step: (0, step)),
            pl.BlockSpec((block, width), lambda step: (step, 0)),
            pl.BlockSpec((8, 128), lambda step: (0, 0)),
        ],
        compiler_params=pltpu.CompilerParams(vmem_limit_bytes=GRANT),
        cost_estimate=pl.CostEstimate(flops=0, bytes_accessed=0, transcendentals=0),
    )(rows, rows_far, grad_produced, grad_produced_far, *wide)


def block_out_kernel(place_ref, returned_ref, hidden_ref, out_ref):
    out_ref[...] = (
        hidden_ref[...] + product(place_ref[...], returned_ref[...], 0, 0)
    ).astype(LOW)


def shards(
    tokens,
    attn_gain,
    query_weight,
    key_weight,
    value_weight,
    output_weight,
    bias_table,
    ffn_gain,
    router_weight,
    expert_in,
    expert_out,
    routes,
    lengths,
    cotangent,
):
    group_rows, width = tokens.shape
    own_rows = cotangent.shape[0]
    heads = bias_table.shape[1]
    buckets = bias_table.shape[0]
    columns = query_weight.shape[1]
    head_size = columns // heads
    sources = lax.axis_size("expert")
    experts = router_weight.shape[1]
    capacity = 2 * own_rows // experts
    slots = experts * capacity
    beyond = sources // (PLANE * LINE)
    router_rows = router_weight.T

    def swap(item):
        return lax.ppermute(item, "shard", [(0, 1), (1, 0)])

    def hop(item, distance):
        return lax.ppermute(item, "expert", [(at, at ^ distance) for at in range(sources)])

    def around(items, stride):
        return tuple(hop(item, stride * (step + 1)) for step, item in enumerate(items))

    def exchange(rows):
        parts = rows.reshape(sources, slots // sources, rows.shape[1])
        came = lax.all_to_all(parts, "expert", split_axis=0, concat_axis=0, tiled=True)
        return came.reshape(rows.shape)

    def beyond_sum(item):
        if beyond == 1:
            return item
        groups = [
            [near + PLANE * LINE * far for far in range(beyond)] for near in range(PLANE * LINE)
        ]
        return lax.psum(item, "expert", axis_index_groups=groups)

    in_own, out_own = expert_in[0], expert_out[0]
    in_came, out_came = swap(in_own), swap(out_own)
    own, other, qkv, probs, normed, mixed = run(
        functools.partial(forward_kernel, head_size=head_size),
        [
            ((own_rows, width), FULL),
            ((own_rows, width), FULL),
            ((group_rows, 3 * columns), LOW),
            ((heads, group_rows, group_rows), LOW),
            ((group_rows, width), LOW),
            ((group_rows, columns), LOW),
        ],
        (
            lengths,
            tokens,
            attn_gain,
            query_weight,
            key_weight,
            value_weight,
            bias_table.T,
            output_weight,
        ),
        scratch=(pltpu.VMEM((group_rows, width), FULL),),
        scalars=1,
    )
    place, hidden, sent, normed_own = run(
        functools.partial(hidden_kernel, experts=experts, capacity=capacity),
        [
            ((slots, own_rows), LOW),
            ((own_rows, width), FULL),
            ((slots, 2 * width), LOW),
            ((own_rows, width), LOW),
        ],
        (routes.reshape(1, own_rows), cotangent, tokens, own, ffn_gain, normed, swap(other)),
    )
    normed_near = around((normed_own,) * 3, 1)
    (
        back,
        grad_back,
        grad_router,
        rows,
        grad_produced,
        active_own,
        active_came,
        grad_pre_own,
        grad_pre_came,
    ) = run(
        expert_kernel,
        [
            ((slots, width), LOW),
            ((slots, width), LOW),
            ((experts, width), FULL),
            ((slots, width), LOW),
            ((slots, width), LOW),
        ]
        + [((slots, in_own.shape[1]), LOW)] * 4,
        (exchange(sent), router_rows, in_own, out_own, in_came, out_came),
        scratch=(
            pltpu.VMEM((2, *in_own.shape), LOW),
            pltpu.VMEM((2, *out_own.shape), LOW),
            pltpu.SemaphoreType.DMA((4,)),
        ),
        raw=(2, 3, 4, 5),
        after=normed_near,
    )
    returned_grads = exchange(grad_back)
    rows_far, grad_produced_far = swap(rows), swap(grad_produced)
    active_far, grad_pre_far = swap(active_came), swap(grad_pre_came)
    small_rows = -(-(experts + 1) // 8) * 8
    attention_own, small_own = run(
        grad_hidden_kernel,
        [((own_rows, width), LOW), ((small_rows, width), FULL)],
        (place, returned_grads, hidden, ffn_gain, cotangent, grad_router),
        after=(rows_far, grad_produced_far, active_far, grad_pre_far),
    )
    attention_came = swap(attention_own)
    part_rows = columns // PLANE
    grad_normed_own, grad_table, back, *parts = run(
        functools.partial(attention_back_kernel, head_size=head_size, bucket_total=buckets),
        [((group_rows, width), LOW), ((heads, buckets), FULL), ((slots, width), LOW)]
        + [((part_rows * (3 + width // group_rows), group_rows), LOW)] * PLANE,
        (
            attention_own,
            attention_came,
            output_weight,
            mixed,
            qkv,
            probs,
            query_weight,
            key_weight,
            value_weight,
            back,
        ),
        scratch=(
            pltpu.VMEM((group_rows, width), LOW),
            pltpu.VMEM((group_rows, 3 * columns), FULL),
            pltpu.VMEM((3 * columns, group_rows), FULL),
            pltpu.VMEM((columns, width), FULL),
        ),
    )
    parts = (parts[0],) + around(parts[1:], 1)
    grad_normed_came = swap(grad_normed_own)
    small_came = swap(small_own)
    normed_far = tuple(swap(item) for item in normed_near)
    late_rows = -(-(heads + 1) // 8) * 8
    grad_tokens, small = run(
        grad_tokens_kernel,
        [((group_rows, width), FULL), ((small_rows + late_rows, width), LOW)],
        (
            tokens,
            attn_gain,
            grad_normed_own,
            grad_normed_came,
            attention_own,
            attention_came,
            small_own,
            small_came,
            grad_table,
        ),
    )
    returned = exchange(back)
    grad_expert_in, grad_expert_out, done = expert_grads(
        rows,
        rows_far,
        grad_produced,
        grad_produced_far,
        active_own,
        active_far,
        grad_pre_own,
        grad_pre_far,
    )
    chunk_rows = 4 * part_rows // LINE
    all_rows = chunk_rows + small_rows + late_rows
    chunks = run(
        sums_kernel,
        [((all_rows, width), LOW)] * LINE,
        parts + normed_near + normed_far + (normed, small),
        scratch=(pltpu.VMEM((part_rows, width), FULL),) * 4,
        after=(returned,),
    )
    (block_out,) = run(
        block_out_kernel, [((own_rows, width), LOW)], (place, returned, hidden)
    )
    chunks = (chunks[0],) + around(chunks[1:], PLANE)
    if beyond == 1:
        whole, chunk = run(
            line_sum_kernel,
            [((all_rows, width), LOW), ((chunk_rows, width), LOW)],
            chunks,
            near=True,
            after=(done,),
        )
    else:
        (whole,) = run(line_sum_kernel, [((all_rows, width), FULL)], chunks)
        whole = beyond_sum(whole).astype(LOW)
        chunk = whole[0:chunk_rows]
    gathered = (whole,) + around((whole,) * 3, 1)
    for item in around((chunk,) * 3, PLANE):
        gathered += (item,) + around((item,) * 3, 1)
    (
        grad_value,
        grad_query,
        grad_key,
        grad_output,
        grad_router,
        grad_ffn_gain,
        grad_attn_gain,
        grad_table,
    ) = run(
        assemble_kernel,
        [((width, columns), FULL)] * 3
        + [((columns, width), FULL), ((experts, width), FULL), ((width,), FULL), ((width,), FULL)]
        + [((heads, buckets), FULL)],
        gathered,
        scratch=(pltpu.VMEM((columns, width), FULL),) * 3,
    )
    grad_router = grad_router.T
    grad_table = grad_table.T
    return (
        block_out,
        grad_tokens,
        grad_attn_gain,
        grad_query,
        grad_key,
        grad_value,
        grad_output,
        grad_table,
        grad_ffn_gain,
        grad_router,
        grad_expert_in[None],
        grad_expert_out[None],
    )


def solution(mesh):
    return jax.shard_map(
        shards,
        mesh=mesh,
        in_specs=(
            P("expert", None),
            P(),
            P(None, "shard"),
            P(None, "shard"),
            P(None, "shard"),
            P("shard", None),
            P(None, "shard"),
            P(),
            P(),
            P("expert", None, "shard"),
            P("expert", "shard", None),
            P(("expert", "shard"), None),
            P("expert", None),
            P(("expert", "shard"), None),
        ),
        out_specs=(
            P(("expert", "shard"), None),
            P("expert", None),
            P(),
            P(None, "shard"),
            P(None, "shard"),
            P(None, "shard"),
            P("shard", None),
            P(None, "shard"),
            P(),
            P(),
            P("expert", None, "shard"),
            P("expert", "shard", None),
        ),
        check_vma=False,
    )
```

```python
import functools

import jax
import jax.numpy as jnp
from jax import lax
from jax.experimental import pallas as pl
from jax.experimental.pallas import tpu as pltpu
from jax.sharding import PartitionSpec as P

EPSILON = 1e-06
BORDERS = (12, 16, 23, 32, 46, 64, 91)
HIGHEST = lax.Precision.HIGHEST
EXCLUDED = -1e30
PLANE = 4
LINE = 4
LOW = jnp.bfloat16
FULL = jnp.float32
MEGABYTE = 1024 * 1024


def inverse_rms(rows):
    return lax.rsqrt(jnp.mean(rows * rows, axis=-1, keepdims=True) + EPSILON)


def norm_back(rows, scale_rows, gain, grad_normed):
    scaled = grad_normed * gain
    grad_rows = scale_rows * scaled - rows * scale_rows**3 * jnp.mean(
        scaled * rows, axis=-1, keepdims=True
    )
    grad_gain = jnp.sum(grad_normed * rows * scale_rows, axis=0, keepdims=True)
    return (grad_rows, grad_gain)


def product(left, right, left_dim=1, right_dim=0, precision=None):
    return lax.dot_general(
        left,
        right,
        (((left_dim,), (right_dim,)), ((), ())),
        precision=precision,
        preferred_element_type=FULL,
    )


def wrapped_buckets(bucket_total, columns):
    column = lax.broadcasted_iota(jnp.int32, (bucket_total, columns), 1)
    offset = jnp.where(column < columns // 2, column, column - columns)
    magnitude = jnp.abs(offset)
    bucket = jnp.minimum(magnitude, 8)
    for border in BORDERS:
        bucket = bucket + (magnitude >= border).astype(jnp.int32)
    bucket = bucket + 16 * (offset > 0).astype(jnp.int32)
    rows = lax.broadcasted_iota(jnp.int32, (bucket_total, columns), 0)
    return (bucket == rows).astype(FULL)


class Fetched:
    def __init__(self, ref, copy):
        self.ref = ref
        self.copy = copy
        self.shape = ref.shape

    def ready(self):
        if self.copy is not None:
            self.copy.wait()
            self.copy = None

    def __getitem__(self, index):
        self.ready()
        return self.ref[index]


class Sent:
    def __init__(self, ref, copy):
        self.ref = ref
        self.copy = copy
        self.shape = ref.shape
        self.dtype = ref.dtype
        self.started = False

    def __getitem__(self, index):
        return self.ref[index]

    def __setitem__(self, index, value):
        self.ref[index] = value

    def send(self):
        if not self.started:
            self.copy.start()
            self.started = True


def run(kernel, outs, operands, scratch=(), scalars=0, raw=(), after=(), near=False):
    count, results = len(operands), len(outs)
    brought = [] if near else [at for at in range(scalars, count) if at not in raw]

    def body(*refs):
        refs = list(refs)
        given = refs[:count]
        rest = refs[count + len(after) :]
        targets, rest = rest[:results], rest[results:]
        if near:
            kernel(*given, *targets, *rest)
            return
        own, rest = rest[: len(scratch)], rest[len(scratch) :]
        buffers, rest = rest[: len(brought)], rest[len(brought) :]
        built, (arrived, left) = rest[:results], rest[results:]
        for slot, (at, buffer) in enumerate(zip(brought, buffers)):
            copy = pltpu.make_async_copy(given[at], buffer, arrived.at[slot])
            copy.start()
            given[at] = Fetched(buffer, copy)
        sent = [
            Sent(buffer, pltpu.make_async_copy(buffer, target, left.at[slot]))
            for slot, (buffer, target) in enumerate(zip(built, targets))
        ]
        kernel(*given, *sent, *own)
        for at in brought:
            given[at].ready()
        for item in sent:
            item.send()
        for item in sent:
            item.copy.wait()

    anywhere = pl.BlockSpec(memory_space=pl.ANY)
    placed = pl.BlockSpec(memory_space=pltpu.VMEM) if near else anywhere
    in_specs = [pl.BlockSpec(memory_space=pltpu.SMEM)] * scalars
    in_specs += [placed] * (count - scalars) + [anywhere] * len(after)
    scratch_shapes = list(scratch)
    if not near:
        scratch_shapes += [pltpu.VMEM(operands[at].shape, operands[at].dtype) for at in brought]
        scratch_shapes += [pltpu.VMEM(shape, dtype) for shape, dtype in outs]
        scratch_shapes += [pltpu.SemaphoreType.DMA((len(brought),))]
        scratch_shapes += [pltpu.SemaphoreType.DMA((results,))]
    return pl.pallas_call(
        body,
        out_shape=[jax.ShapeDtypeStruct(shape, dtype) for shape, dtype in outs],
        in_specs=in_specs,
        out_specs=[placed] * results,
        scratch_shapes=scratch_shapes,
        compiler_params=pltpu.CompilerParams(vmem_limit_bytes=(4 if near else 56) * MEGABYTE),
        cost_estimate=pl.CostEstimate(flops=0, bytes_accessed=0, transcendentals=0),
    )(*operands, *after)


def placed_rows(chosen, experts, capacity, slots):
    own_rows = chosen.shape[1]
    picked = chosen == lax.broadcasted_iota(jnp.int32, (experts, own_rows), 0)
    picked_float = picked.astype(FULL)
    earlier = lax.broadcasted_iota(jnp.int32, (own_rows, own_rows), 0) < lax.broadcasted_iota(
        jnp.int32, (own_rows, own_rows), 1
    )
    ranks = product(picked_float.astype(LOW), earlier.astype(FULL).astype(LOW))
    rank = jnp.sum(ranks * picked_float, axis=0, keepdims=True)
    target = chosen * capacity + rank.astype(jnp.int32)
    place = target == lax.broadcasted_iota(jnp.int32, (slots, own_rows), 0)
    return place.astype(FULL).astype(LOW)


def forward_kernel(
    lengths_ref,
    tokens_ref,
    gain_ref,
    query_ref,
    key_ref,
    value_ref,
    table_ref,
    output_ref,
    own_ref,
    other_ref,
    qkv_ref,
    probs_ref,
    normed_turned_ref,
    mixed_ref,
    whole_ref,
    *,
    head_size,
):
    group_rows = tokens_ref.shape[0]
    own_rows = own_ref.shape[0]
    heads, buckets = table_ref.shape
    columns = heads * head_size
    scale = head_size ** (-0.5)
    half = lax.axis_index("shard")
    own_at = pl.multiple_of(half * own_rows, own_rows)
    other_at = pl.multiple_of((1 - half) * own_rows, own_rows)
    inputs = tokens_ref[...].astype(FULL)
    normed = inputs * inverse_rms(inputs) * gain_ref[...].reshape(1, -1)
    whole_ref[...] = normed
    normed_turned_ref[0:own_rows, :] = whole_ref[pl.ds(own_at, own_rows), :].astype(LOW)
    normed_turned_ref[own_rows:, :] = whole_ref[pl.ds(other_at, own_rows), :].astype(LOW)
    normed = normed.astype(LOW)
    queries = product(normed, query_ref[...]).astype(LOW)
    keys = product(normed, key_ref[...]).astype(LOW)
    values = product(normed, value_ref[...]).astype(LOW)
    qkv_ref[:, 0:columns] = queries
    qkv_ref[:, columns : 2 * columns] = keys
    qkv_ref[:, 2 * columns : 3 * columns] = values
    qkv_ref.send()
    normed_turned_ref.send()
    per_offset = product(
        table_ref[...], wrapped_buckets(buckets, group_rows), 1, 0, HIGHEST
    )
    row_at = lax.broadcasted_iota(jnp.int32, (group_rows, group_rows), 0)
    column_at = lax.broadcasted_iota(jnp.int32, (group_rows, group_rows), 1)
    row_part = jnp.zeros((group_rows, group_rows), jnp.int32)
    column_part = jnp.zeros((group_rows, group_rows), jnp.int32)
    end = 0
    for part in range(lengths_ref.shape[1] - 1):
        end = end + lengths_ref[0, part]
        row_part = row_part + (row_at >= end).astype(jnp.int32)
        column_part = column_part + (column_at >= end).astype(jnp.int32)
    same = row_part == column_part
    mixed_parts = []
    for head in range(heads):
        here = slice(head * head_size, (head + 1) * head_size)
        bias = pltpu.roll(
            jnp.broadcast_to(per_offset[head : head + 1, :], (group_rows, group_rows)),
            0,
            1,
            stride=1,
            stride_axis=0,
        )
        scores = product(queries[:, here], keys[:, here], 1, 1)
        scores = jnp.where(same, scores * scale + bias, EXCLUDED)
        raised = jnp.exp(scores - jnp.max(scores, axis=-1, keepdims=True))
        probs = raised * (1.0 / jnp.sum(raised, axis=-1, keepdims=True))
        probs = probs.astype(LOW)
        probs_ref[head] = probs
        mixed_parts.append(product(probs, values[:, here]))
    probs_ref.send()
    mixed = jnp.concatenate(mixed_parts, axis=1).astype(LOW)
    mixed_ref[...] = mixed
    mixed_ref.send()
    whole_ref[...] = product(mixed, output_ref[...])
    own_ref[...] = whole_ref[pl.ds(own_at, own_rows), :]
    other_ref[...] = whole_ref[pl.ds(other_at, own_rows), :]


def hidden_kernel(
    routes_ref,
    cotangent_ref,
    tokens_ref,
    own_ref,
    gain_ref,
    normed_ref,
    came_ref,
    place_ref,
    hidden_ref,
    sent_ref,
    normed_own_ref,
    *,
    experts,
    capacity,
):
    own_rows, width = own_ref.shape
    slots = place_ref.shape[0]
    place = placed_rows(routes_ref[...], experts, capacity, slots)
    place_ref[...] = place
    place_ref.send()
    sent_ref[:, width:] = product(place, cotangent_ref[...]).astype(LOW)
    own_at = pl.multiple_of(lax.axis_index("shard") * own_rows, own_rows)
    inputs = tokens_ref[pl.ds(own_at, own_rows), :].astype(FULL)
    hidden = inputs + (own_ref[...] + came_ref[...])
    normed = (hidden * inverse_rms(hidden) * gain_ref[...].reshape(1, -1)).astype(LOW)
    sent_ref[:, 0:width] = product(place, normed).astype(LOW)
    sent_ref.send()
    hidden_ref[...] = hidden
    normed_own_ref[...] = normed_ref[0:own_rows, :]


def expert_kernel(
    arrived_ref,
    router_ref,
    in_own_ref,
    out_own_ref,
    in_came_ref,
    out_came_ref,
    back_ref,
    grad_back_ref,
    grad_router_ref,
    rows_ref,
    grad_produced_ref,
    active_own_ref,
    active_came_ref,
    grad_pre_own_ref,
    grad_pre_came_ref,
    in_held_ref,
    out_held_ref,
    arrived,
):
    width, units = in_own_ref.shape
    copies = [
        pltpu.make_async_copy(source, target, arrived.at[at])
        for at, (source, target) in enumerate(
            (
                (in_own_ref, in_held_ref.at[0]),
                (out_own_ref, out_held_ref.at[0]),
                (in_came_ref, in_held_ref.at[1]),
                (out_came_ref, out_held_ref.at[1]),
            )
        )
    ]
    for copy in copies:
        copy.start()
    rows = arrived_ref[:, 0:width]
    grads = arrived_ref[:, width:].astype(FULL)
    rows_ref[...] = rows
    rows_ref.send()
    logits = product(rows, router_ref[...], 1, 1)
    raised = jnp.exp(logits - jnp.max(logits, axis=-1, keepdims=True))
    chances = raised * (1.0 / jnp.sum(raised, axis=-1, keepdims=True))
    chosen = lax.broadcasted_iota(jnp.int32, chances.shape, 1) == lax.axis_index("expert")
    gate = jnp.sum(jnp.where(chosen, chances, 0.0), axis=1, keepdims=True)
    grad_produced = (gate * grads).astype(LOW)
    grad_produced_ref[...] = grad_produced
    grad_produced_ref.send()
    produced = 0.0
    grad_rows = 0.0
    block = 512
    for source in range(2):
        copies[2 * source].wait()
        copies[2 * source + 1].wait()
        active_ref = (active_own_ref, active_came_ref)[source]
        grad_pre_ref = (grad_pre_own_ref, grad_pre_came_ref)[source]
        for first in range(0, units, block):
            here = slice(first, first + block)
            in_block = in_held_ref[source, :, here]
            out_block = out_held_ref[source, here, :]
            pre = product(rows, in_block)
            grad_active = product(grad_produced, out_block, 1, 1)
            steep = 1.0 / (1.0 + 0.2316419 * jnp.abs(pre))
            density = jnp.exp(-0.5 * pre * pre) * 0.3989422804014327
            tail = 1.330274429
            for factor in (-1.821255978, 1.781477937, -0.356563782, 0.319381530):
                tail = tail * steep + factor
            tail = tail * steep * density
            cumulative = jnp.where(pre >= 0.0, 1.0 - tail, tail)
            active = (pre * cumulative).astype(LOW)
            grad_pre = (grad_active * (cumulative + pre * density)).astype(LOW)
            active_ref[:, here] = active
            grad_pre_ref[:, here] = grad_pre
            produced = produced + product(active, out_block)
            grad_rows = grad_rows + product(grad_pre, in_block, 1, 1)
        active_ref.send()
        grad_pre_ref.send()
    produced = produced.astype(LOW).astype(FULL)
    grad_gate = jnp.sum(grads * produced, axis=1, keepdims=True)
    grad_logits = (grad_gate * chances * (chosen.astype(FULL) - gate)).astype(LOW)
    grad_back_ref[...] = (grad_rows + product(grad_logits, router_ref[...])).astype(LOW)
    grad_back_ref.send()
    back_ref[...] = (gate * produced).astype(LOW)
    grad_router_ref[...] = product(grad_logits, rows, 0, 0)


def halves(own_rows):
    half = lax.axis_index("shard")
    own_at = pl.multiple_of(half * own_rows, own_rows)
    other_at = pl.multiple_of((1 - half) * own_rows, own_rows)
    return (own_at, other_at)


def attention_back_kernel(
    place_own_ref,
    place_came_ref,
    hidden_own_ref,
    hidden_came_ref,
    gain_ref,
    cotangent_own_ref,
    cotangent_came_ref,
    returned_own_ref,
    returned_came_ref,
    output_ref,
    mixed_ref,
    qkv_ref,
    probs_ref,
    attention_ref,
    grad_ffn_ref,
    grad_low_ref,
    grad_table_ref,
    part_ref,
    part_one_ref,
    part_two_ref,
    part_three_ref,
    grads_ref,
    turned_ref,
    output_grad_ref,
    *,
    head_size,
    bucket_total,
):
    own_rows, width = hidden_own_ref.shape
    group_rows = 2 * own_rows
    heads = probs_ref.shape[0]
    columns = heads * head_size
    scale = head_size ** (-0.5)
    own_at, other_at = halves(own_rows)
    gain = gain_ref[...].reshape(1, -1)
    grad_gains = []
    for at, place, rows, cotangent, returned in (
        (own_at, place_own_ref, hidden_own_ref, cotangent_own_ref, returned_own_ref),
        (other_at, place_came_ref, hidden_came_ref, cotangent_came_ref, returned_came_ref),
    ):
        hidden = rows[...]
        grads = product(place[...], returned[...], 0, 0)
        grad_rows, grad_gain = norm_back(hidden, inverse_rms(hidden), gain, grads)
        grad_rows = cotangent[...].astype(FULL) + grad_rows
        attention_ref[pl.ds(at, own_rows), :] = grad_rows.astype(LOW)
        grad_gains.append(grad_gain)
    grad_ffn_ref[...] = grad_gains[0] + grad_gains[1]
    attention_ref.send()
    grad_mixed = product(attention_ref[...], output_ref[...], 1, 1).astype(LOW)
    output_grad_ref[...] = product(mixed_ref[...], attention_ref[...], 0, 0)
    reversal = (
        lax.broadcasted_iota(jnp.int32, (group_rows, group_rows), 0)
        + lax.broadcasted_iota(jnp.int32, (group_rows, group_rows), 1)
        == group_rows - 1
    )
    reversal = reversal.astype(FULL).astype(LOW)
    grad_queries, grad_keys, grad_values, sums = [], [], [], []
    for head in range(heads):
        first = head * head_size
        queries = qkv_ref[:, first : first + head_size]
        keys = qkv_ref[:, columns + first : columns + first + head_size]
        values = qkv_ref[:, 2 * columns + first : 2 * columns + first + head_size]
        probs = probs_ref[head].astype(FULL)
        grad_head = grad_mixed[:, first : first + head_size]
        grad_probs = product(grad_head, values, 1, 1)
        inner = jnp.sum(probs * grad_probs, axis=-1, keepdims=True)
        grad_scores = probs * (grad_probs - inner)
        upper = grad_scores.astype(LOW)
        rest = (grad_scores - upper.astype(FULL)).astype(LOW)
        backwards = product(reversal, upper) + product(reversal, rest)
        aligned = pltpu.roll(backwards, 1, 1, stride=1, stride_axis=0)
        sums.append(jnp.sum(aligned, axis=0, keepdims=True))
        grad_queries.append(product(upper, keys) * scale)
        grad_keys.append(product(upper, queries, 0, 0) * scale)
        grad_values.append(product(probs_ref[head], grad_head, 0, 0))
    grad_table_ref[...] = product(
        jnp.concatenate(sums, axis=0), wrapped_buckets(bucket_total, group_rows), 1, 1, HIGHEST
    )
    grad_queries = jnp.concatenate(grad_queries, axis=1)
    grad_keys = jnp.concatenate(grad_keys, axis=1)
    grad_values = jnp.concatenate(grad_values, axis=1)
    grads_ref[:, 0:columns] = grad_values
    grads_ref[:, columns : 2 * columns] = grad_queries
    grads_ref[:, 2 * columns : 3 * columns] = grad_keys
    grad_low_ref[...] = grads_ref[...].astype(LOW)
    grad_low_ref.send()
    turned_ref[:, 0:own_rows] = grads_ref[pl.ds(own_at, own_rows), :].T
    turned_ref[:, own_rows:] = grads_ref[pl.ds(other_at, own_rows), :].T
    mine = lax.rem(lax.axis_index("expert"), PLANE)
    rows = columns // PLANE
    refs = (part_ref, part_one_ref, part_two_ref, part_three_ref)
    for other, ref in enumerate(refs):
        for weight in range(3):
            at = pl.multiple_of((mine ^ other) * rows + weight * columns, 16)
            ref[weight * rows : (weight + 1) * rows, :] = turned_ref[pl.ds(at, rows), :].astype(
                LOW
            )
        at = pl.multiple_of((mine ^ other) * rows, 16)
        quarter = output_grad_ref[pl.ds(at, rows), :].astype(LOW)
        for piece in range(width // group_rows):
            ref[(3 + piece) * rows : (4 + piece) * rows, :] = quarter[
                :, piece * group_rows : (piece + 1) * group_rows
            ]
        ref.send()


def grad_tokens_kernel(
    tokens_ref,
    gain_ref,
    attention_ref,
    router_own_ref,
    router_came_ref,
    ffn_ref,
    table_ref,
    back_ref,
    grads_own_ref,
    value_own_ref,
    query_own_ref,
    key_own_ref,
    value_came_ref,
    query_came_ref,
    key_came_ref,
    grads_came_ref,
    grad_tokens_ref,
    small_ref,
    back_out_ref,
):
    back_out_ref[...] = back_ref[...]
    back_out_ref.send()
    width, columns = value_own_ref.shape
    experts = router_own_ref.shape[0]
    heads, buckets = table_ref.shape
    sums = []
    for grads, weights in (
        (grads_own_ref, (value_own_ref, query_own_ref, key_own_ref)),
        (grads_came_ref, (value_came_ref, query_came_ref, key_came_ref)),
    ):
        total = 0.0
        for at, ref in enumerate(weights):
            part = grads[:, at * columns : (at + 1) * columns]
            total = total + product(part, ref[...], 1, 1)
        sums.append(total)
    grad_normed = sums[0] + sums[1]
    inputs = tokens_ref[...].astype(FULL)
    grad_rows, grad_gain = norm_back(
        inputs, inverse_rms(inputs), gain_ref[...].reshape(1, -1), grad_normed
    )
    grad_tokens_ref[...] = grad_rows + attention_ref[...].astype(FULL)
    table = jnp.concatenate([table_ref[...], jnp.zeros((heads, width - buckets), FULL)], axis=1)
    early = -(-(experts + 1) // 8) * 8
    small_ref[...] = jnp.concatenate(
        [
            router_own_ref[...] + router_came_ref[...],
            ffn_ref[...],
            jnp.zeros((early - experts - 1, width), FULL),
            grad_gain,
            table,
            jnp.zeros((small_ref.shape[0] - early - heads - 1, width), FULL),
        ],
        axis=0,
    ).astype(small_ref.dtype)


def line_chunks(totals, refs, total_refs, shared=()):
    mine = lax.rem(lax.axis_index("expert") // PLANE, LINE)
    for total, total_ref in zip(totals, total_refs):
        total_ref[...] = total
    for other, ref in enumerate(refs):
        chunks = []
        for total_ref in total_refs:
            rows = total_ref.shape[0] // LINE
            at = pl.multiple_of((mine ^ other) * rows, 8)
            chunks.append(total_ref[pl.ds(at, rows), :])
        ref[...] = jnp.concatenate(chunks + list(shared), axis=0).astype(ref.dtype)
        ref.send()


def sums_kernel(*refs):
    parts, nears, fars, normed_ref, small_ref = refs[0:4], refs[4:7], refs[7:10], *refs[10:12]
    outs, total_refs = refs[12:16], refs[16:20]
    own_rows = normed_ref.shape[0] // 2
    rows = total_refs[0].shape[0]
    pieces = normed_ref.shape[1] // parts[0].shape[1]
    output = 0.0
    weights = 0.0
    for at, part in enumerate(parts):
        output = output + jnp.concatenate(
            [part[(3 + piece) * rows : (4 + piece) * rows, :] for piece in range(pieces)], axis=1
        ).astype(FULL)
        near = nears[at - 1][...] if at else normed_ref[0:own_rows]
        far = fars[at - 1][...] if at else normed_ref[own_rows:]
        weights = weights + product(part[0 : 3 * rows, 0:own_rows], near)
        weights = weights + product(part[0 : 3 * rows, own_rows:], far)
    totals = (weights[0:rows], weights[rows : 2 * rows], weights[2 * rows :], output)
    line_chunks(totals, outs, total_refs, (small_ref[...].astype(FULL),))


def summed(refs, rows=slice(None)):
    near = refs[0][rows, :].astype(FULL) + refs[1][rows, :].astype(FULL)
    far = refs[2][rows, :].astype(FULL) + refs[3][rows, :].astype(FULL)
    return near + far


def line_sum_kernel(*refs):
    total = summed(refs[0:LINE])
    for out_ref in refs[LINE:]:
        out_ref[...] = total[0 : out_ref.shape[0]].astype(out_ref.dtype)


def assemble_kernel(*refs):
    chunk_refs = refs[0 : PLANE * LINE]
    value_ref, query_ref, key_ref, output_ref, router_ref, ffn_ref, attn_ref, table_ref = refs[
        PLANE * LINE : -3
    ]
    totals = refs[-3:] + (output_ref.ref,)
    member = lax.rem(lax.axis_index("expert"), PLANE)
    floor = lax.rem(lax.axis_index("expert") // PLANE, LINE)
    rows = output_ref.shape[0] // PLANE // LINE
    for along in range(LINE):
        for across in range(PLANE):
            chunk = chunk_refs[along * PLANE + across][0 : 4 * rows, :].astype(FULL)
            at = pl.multiple_of(((member ^ across) * LINE + (floor ^ along)) * rows, 8)
            for weight, total_ref in enumerate(totals):
                total_ref[pl.ds(at, rows), :] = chunk[weight * rows : (weight + 1) * rows]
    output_ref.send()
    for total_ref, ref in zip(totals, (value_ref, query_ref, key_ref)):
        ref[...] = total_ref[...].T
        ref.send()
    small = summed(chunk_refs[0:PLANE], slice(4 * rows, None))
    experts = router_ref.shape[0]
    heads, buckets = table_ref.shape
    late = -(-(experts + 1) // 8) * 8
    router_ref[...] = small[0:experts]
    ffn_ref[...] = small[experts : experts + 1].reshape(-1)
    attn_ref[...] = small[late : late + 1].reshape(-1)
    table_ref[...] = small[late + 1 : late + 1 + heads, 0:buckets]


def expert_grads_kernel(
    rows_ref,
    rows_far_ref,
    grad_produced_ref,
    grad_produced_far_ref,
    active_ref,
    active_far_ref,
    grad_pre_ref,
    grad_pre_far_ref,
    grad_in_ref,
    grad_out_ref,
    done_ref,
):
    done_ref[...] = jnp.zeros_like(done_ref)
    grad_in_ref[...] = product(rows_ref[...], grad_pre_ref[...], 0, 0) + product(
        rows_far_ref[...], grad_pre_far_ref[...], 0, 0
    )
    grad_out_ref[...] = product(active_ref[...], grad_produced_ref[...], 0, 0) + product(
        active_far_ref[...], grad_produced_far_ref[...], 0, 0
    )


def expert_grads(rows, rows_far, grad_produced, grad_produced_far, *wide):
    slots, width = rows.shape
    units = wide[0].shape[1]
    block = 768
    fixed = pl.BlockSpec((slots, width), lambda step: (0, 0))
    moving = pl.BlockSpec((slots, block), lambda step: (0, step))
    return pl.pallas_call(
        expert_grads_kernel,
        grid=(units // block,),
        out_shape=[
            jax.ShapeDtypeStruct((width, units), FULL),
            jax.ShapeDtypeStruct((units, width), FULL),
            jax.ShapeDtypeStruct((8, 128), FULL),
        ],
        in_specs=[fixed] * 4 + [moving] * 4,
        out_specs=[
            pl.BlockSpec((width, block), lambda step: (0, step)),
            pl.BlockSpec((block, width), lambda step: (step, 0)),
            pl.BlockSpec((8, 128), lambda step: (0, 0)),
        ],
        compiler_params=pltpu.CompilerParams(vmem_limit_bytes=56 * MEGABYTE),
        cost_estimate=pl.CostEstimate(flops=0, bytes_accessed=0, transcendentals=0),
    )(rows, rows_far, grad_produced, grad_produced_far, *wide)


def block_out_kernel(place_ref, returned_ref, hidden_ref, out_ref):
    out_ref[...] = (
        hidden_ref[...] + product(place_ref[...], returned_ref[...], 0, 0)
    ).astype(LOW)


def shards(
    tokens,
    attn_gain,
    query_weight,
    key_weight,
    value_weight,
    output_weight,
    bias_table,
    ffn_gain,
    router_weight,
    expert_in,
    expert_out,
    routes,
    lengths,
    cotangent,
):
    group_rows, width = tokens.shape
    own_rows = cotangent.shape[0]
    heads = bias_table.shape[1]
    buckets = bias_table.shape[0]
    columns = query_weight.shape[1]
    head_size = columns // heads
    sources = lax.axis_size("expert")
    experts = router_weight.shape[1]
    capacity = 2 * own_rows // experts
    slots = experts * capacity
    beyond = sources // (PLANE * LINE)
    router_rows = router_weight.T

    def swap(item):
        return lax.ppermute(item, "shard", [(0, 1), (1, 0)])

    def hop(item, distance):
        return lax.ppermute(item, "expert", [(at, at ^ distance) for at in range(sources)])

    def around(items, stride):
        return tuple(hop(item, stride * (step + 1)) for step, item in enumerate(items))

    def exchange(rows):
        parts = rows.reshape(sources, slots // sources, rows.shape[1])
        came = lax.all_to_all(parts, "expert", split_axis=0, concat_axis=0, tiled=True)
        return came.reshape(rows.shape)

    def beyond_sum(item):
        if beyond == 1:
            return item
        groups = [
            [near + PLANE * LINE * far for far in range(beyond)] for near in range(PLANE * LINE)
        ]
        return lax.psum(item, "expert", axis_index_groups=groups)

    in_own, out_own = expert_in[0], expert_out[0]
    in_came, out_came = swap(in_own), swap(out_own)
    own, other, qkv, probs, normed, mixed = run(
        functools.partial(forward_kernel, head_size=head_size),
        [
            ((own_rows, width), FULL),
            ((own_rows, width), FULL),
            ((group_rows, 3 * columns), LOW),
            ((heads, group_rows, group_rows), LOW),
            ((group_rows, width), LOW),
            ((group_rows, columns), LOW),
        ],
        (
            lengths,
            tokens,
            attn_gain,
            query_weight,
            key_weight,
            value_weight,
            bias_table.T,
            output_weight,
        ),
        scratch=(pltpu.VMEM((group_rows, width), FULL),),
        scalars=1,
    )
    place, hidden, sent, normed_own = run(
        functools.partial(hidden_kernel, experts=experts, capacity=capacity),
        [
            ((slots, own_rows), LOW),
            ((own_rows, width), FULL),
            ((slots, 2 * width), LOW),
            ((own_rows, width), LOW),
        ],
        (routes.reshape(1, own_rows), cotangent, tokens, own, ffn_gain, normed, swap(other)),
    )
    normed_near = around((normed_own,) * 3, 1)
    (
        back,
        grad_back,
        grad_router,
        rows,
        grad_produced,
        active_own,
        active_came,
        grad_pre_own,
        grad_pre_came,
    ) = run(
        expert_kernel,
        [
            ((slots, width), LOW),
            ((slots, width), LOW),
            ((experts, width), FULL),
            ((slots, width), LOW),
            ((slots, width), LOW),
        ]
        + [((slots, in_own.shape[1]), LOW)] * 4,
        (exchange(sent), router_rows, in_own, out_own, in_came, out_came),
        scratch=(
            pltpu.VMEM((2, *in_own.shape), LOW),
            pltpu.VMEM((2, *out_own.shape), LOW),
            pltpu.SemaphoreType.DMA((4,)),
        ),
        raw=(2, 3, 4, 5),
        after=normed_near,
    )
    returned_grads = exchange(grad_back)
    rows_far, grad_produced_far = swap(rows), swap(grad_produced)
    active_far, grad_pre_far = swap(active_came), swap(grad_pre_came)
    grad_router_came = swap(grad_router)
    place_came, hidden_came, cotangent_came = swap(place), swap(hidden), swap(cotangent)
    small_rows = -(-(experts + 1) // 8) * 8
    part_rows = columns // PLANE
    attention, grad_ffn, grads_low, grad_table, *parts = run(
        functools.partial(attention_back_kernel, head_size=head_size, bucket_total=buckets),
        [
            ((group_rows, width), LOW),
            ((1, width), FULL),
            ((group_rows, 3 * columns), LOW),
            ((heads, buckets), FULL),
        ]
        + [((part_rows * (3 + width // group_rows), group_rows), LOW)] * PLANE,
        (
            place,
            place_came,
            hidden,
            hidden_came,
            ffn_gain,
            cotangent,
            cotangent_came,
            returned_grads,
            swap(returned_grads),
            output_weight,
            mixed,
            qkv,
            probs,
        ),
        scratch=(
            pltpu.VMEM((group_rows, 3 * columns), FULL),
            pltpu.VMEM((3 * columns, group_rows), FULL),
            pltpu.VMEM((columns, width), FULL),
        ),
        after=(
            rows_far,
            grad_produced_far,
            active_far,
            grad_pre_far,
            grad_router_came,
        ),
    )
    parts = (parts[0],) + around(parts[1:], 1)
    grads_came = swap(grads_low)
    weights = (value_weight, query_weight, key_weight)
    weights_came = tuple(swap(item) for item in weights)
    normed_far = tuple(swap(item) for item in normed_near)
    late_rows = -(-(heads + 1) // 8) * 8
    grad_tokens, small, back = run(
        grad_tokens_kernel,
        [
            ((group_rows, width), FULL),
            ((small_rows + late_rows, width), LOW),
            ((slots, width), LOW),
        ],
        (
            tokens,
            attn_gain,
            attention,
            grad_router,
            grad_router_came,
            grad_ffn,
            grad_table,
            back,
            grads_low,
            *weights,
            *weights_came,
            grads_came,
        ),
    )
    returned = exchange(back)
    grad_expert_in, grad_expert_out, done = expert_grads(
        rows,
        rows_far,
        grad_produced,
        grad_produced_far,
        active_own,
        active_far,
        grad_pre_own,
        grad_pre_far,
    )
    chunk_rows = 4 * part_rows // LINE
    all_rows = chunk_rows + small_rows + late_rows
    chunks = run(
        sums_kernel,
        [((all_rows, width), LOW)] * LINE,
        parts + normed_near + normed_far + (normed, small),
        scratch=(pltpu.VMEM((part_rows, width), FULL),) * 4,
    )
    (block_out,) = run(
        block_out_kernel, [((own_rows, width), LOW)], (place, returned, hidden)
    )
    chunks = (chunks[0],) + around(chunks[1:], PLANE)
    if beyond == 1:
        whole, chunk = run(
            line_sum_kernel,
            [((all_rows, width), LOW), ((chunk_rows, width), LOW)],
            chunks,
            near=True,
            after=(done,),
        )
    else:
        (whole,) = run(line_sum_kernel, [((all_rows, width), FULL)], chunks)
        whole = beyond_sum(whole).astype(LOW)
        chunk = whole[0:chunk_rows]
    gathered = (whole,) + around((whole,) * 3, 1)
    for item in around((chunk,) * 3, PLANE):
        gathered += (item,) + around((item,) * 3, 1)
    (
        grad_value,
        grad_query,
        grad_key,
        grad_output,
        grad_router,
        grad_ffn_gain,
        grad_attn_gain,
        grad_table,
    ) = run(
        assemble_kernel,
        [((width, columns), FULL)] * 3
        + [((columns, width), FULL), ((experts, width), FULL), ((width,), FULL), ((width,), FULL)]
        + [((heads, buckets), FULL)],
        gathered,
        scratch=(pltpu.VMEM((columns, width), FULL),) * 3,
        after=(block_out,),
    )
    grad_router = grad_router.T
    grad_table = grad_table.T
    return (
        block_out,
        grad_tokens,
        grad_attn_gain,
        grad_query,
        grad_key,
        grad_value,
        grad_output,
        grad_table,
        grad_ffn_gain,
        grad_router,
        grad_expert_in[None],
        grad_expert_out[None],
    )


def solution(mesh):
    return jax.shard_map(
        shards,
        mesh=mesh,
        in_specs=(
            P("expert", None),
            P(),
            P(None, "shard"),
            P(None, "shard"),
            P(None, "shard"),
            P("shard", None),
            P(None, "shard"),
            P(),
            P(),
            P("expert", None, "shard"),
            P("expert", "shard", None),
            P(("expert", "shard"), None),
            P("expert", None),
            P(("expert", "shard"), None),
        ),
        out_specs=(
            P(("expert", "shard"), None),
            P("expert", None),
            P(),
            P(None, "shard"),
            P(None, "shard"),
            P(None, "shard"),
            P("shard", None),
            P(None, "shard"),
            P(),
            P(),
            P("expert", None, "shard"),
            P("expert", "shard", None),
        ),
        check_vma=False,
    )
```

```python
import functools

import jax
import jax.numpy as jnp
from jax import lax
from jax.experimental import pallas as pl
from jax.experimental.pallas import tpu as pltpu
from jax.sharding import PartitionSpec as P

EPSILON = 1e-06
BORDERS = (12, 16, 23, 32, 46, 64, 91)
HIGHEST = lax.Precision.HIGHEST
EXCLUDED = -1e30
PLANE = 4
LINE = 4
LOW = jnp.bfloat16
FULL = jnp.float32
MEGABYTE = 1024 * 1024


def inverse_rms(rows):
    return lax.rsqrt(jnp.mean(rows * rows, axis=-1, keepdims=True) + EPSILON)


def norm_back(rows, scale_rows, gain, grad_normed):
    scaled = grad_normed * gain
    grad_rows = scale_rows * scaled - rows * scale_rows**3 * jnp.mean(
        scaled * rows, axis=-1, keepdims=True
    )
    grad_gain = jnp.sum(grad_normed * rows * scale_rows, axis=0, keepdims=True)
    return (grad_rows, grad_gain)


def product(left, right, left_dim=1, right_dim=0, precision=None):
    return lax.dot_general(
        left,
        right,
        (((left_dim,), (right_dim,)), ((), ())),
        precision=precision,
        preferred_element_type=FULL,
    )


def wrapped_buckets(bucket_total, columns):
    column = lax.broadcasted_iota(jnp.int32, (bucket_total, columns), 1)
    offset = jnp.where(column < columns // 2, column, column - columns)
    magnitude = jnp.abs(offset)
    bucket = jnp.minimum(magnitude, 8)
    for border in BORDERS:
        bucket = bucket + (magnitude >= border).astype(jnp.int32)
    bucket = bucket + 16 * (offset > 0).astype(jnp.int32)
    rows = lax.broadcasted_iota(jnp.int32, (bucket_total, columns), 0)
    return (bucket == rows).astype(FULL)


class Fetched:
    def __init__(self, ref, copy):
        self.ref = ref
        self.copy = copy
        self.shape = ref.shape

    def ready(self):
        if self.copy is not None:
            self.copy.wait()
            self.copy = None

    def __getitem__(self, index):
        self.ready()
        return self.ref[index]


class Sent:
    def __init__(self, ref, copy):
        self.ref = ref
        self.copy = copy
        self.shape = ref.shape
        self.dtype = ref.dtype
        self.started = False

    def __getitem__(self, index):
        return self.ref[index]

    def __setitem__(self, index, value):
        self.ref[index] = value

    def send(self):
        if not self.started:
            self.copy.start()
            self.started = True


def run(kernel, outs, operands, scratch=(), scalars=0, raw=(), after=(), near=False):
    count, results = len(operands), len(outs)
    brought = [] if near else [at for at in range(scalars, count) if at not in raw]

    def body(*refs):
        refs = list(refs)
        given = refs[:count]
        rest = refs[count + len(after) :]
        targets, rest = rest[:results], rest[results:]
        if near:
            kernel(*given, *targets, *rest)
            return
        own, rest = rest[: len(scratch)], rest[len(scratch) :]
        buffers, rest = rest[: len(brought)], rest[len(brought) :]
        built, (arrived, left) = rest[:results], rest[results:]
        for slot, (at, buffer) in enumerate(zip(brought, buffers)):
            copy = pltpu.make_async_copy(given[at], buffer, arrived.at[slot])
            copy.start()
            given[at] = Fetched(buffer, copy)
        sent = [
            Sent(buffer, pltpu.make_async_copy(buffer, target, left.at[slot]))
            for slot, (buffer, target) in enumerate(zip(built, targets))
        ]
        kernel(*given, *sent, *own)
        for at in brought:
            given[at].ready()
        for item in sent:
            item.send()
        for item in sent:
            item.copy.wait()

    anywhere = pl.BlockSpec(memory_space=pl.ANY)
    placed = pl.BlockSpec(memory_space=pltpu.VMEM) if near else anywhere
    in_specs = [pl.BlockSpec(memory_space=pltpu.SMEM)] * scalars
    in_specs += [placed] * (count - scalars) + [anywhere] * len(after)
    scratch_shapes = list(scratch)
    if not near:
        scratch_shapes += [pltpu.VMEM(operands[at].shape, operands[at].dtype) for at in brought]
        scratch_shapes += [pltpu.VMEM(shape, dtype) for shape, dtype in outs]
        scratch_shapes += [pltpu.SemaphoreType.DMA((len(brought),))]
        scratch_shapes += [pltpu.SemaphoreType.DMA((results,))]
    return pl.pallas_call(
        body,
        out_shape=[jax.ShapeDtypeStruct(shape, dtype) for shape, dtype in outs],
        in_specs=in_specs,
        out_specs=[placed] * results,
        scratch_shapes=scratch_shapes,
        compiler_params=pltpu.CompilerParams(vmem_limit_bytes=(4 if near else 56) * MEGABYTE),
        cost_estimate=pl.CostEstimate(flops=0, bytes_accessed=0, transcendentals=0),
    )(*operands, *after)


def placed_rows(chosen, experts, capacity, slots):
    own_rows = chosen.shape[1]
    picked = chosen == lax.broadcasted_iota(jnp.int32, (experts, own_rows), 0)
    picked_float = picked.astype(FULL)
    earlier = lax.broadcasted_iota(jnp.int32, (own_rows, own_rows), 0) < lax.broadcasted_iota(
        jnp.int32, (own_rows, own_rows), 1
    )
    ranks = product(picked_float.astype(LOW), earlier.astype(FULL).astype(LOW))
    rank = jnp.sum(ranks * picked_float, axis=0, keepdims=True)
    target = chosen * capacity + rank.astype(jnp.int32)
    place = target == lax.broadcasted_iota(jnp.int32, (slots, own_rows), 0)
    return place.astype(FULL).astype(LOW)


def forward_kernel(
    lengths_ref,
    tokens_ref,
    gain_ref,
    query_ref,
    key_ref,
    value_ref,
    table_ref,
    output_ref,
    own_ref,
    other_ref,
    qkv_ref,
    probs_ref,
    normed_turned_ref,
    mixed_ref,
    whole_ref,
    *,
    head_size,
):
    group_rows = tokens_ref.shape[0]
    own_rows = own_ref.shape[0]
    heads, buckets = table_ref.shape
    columns = heads * head_size
    scale = head_size ** (-0.5)
    half = lax.axis_index("shard")
    own_at = pl.multiple_of(half * own_rows, own_rows)
    other_at = pl.multiple_of((1 - half) * own_rows, own_rows)
    inputs = tokens_ref[...].astype(FULL)
    normed = inputs * inverse_rms(inputs) * gain_ref[...].reshape(1, -1)
    whole_ref[...] = normed
    normed_turned_ref[0:own_rows, :] = whole_ref[pl.ds(own_at, own_rows), :].astype(LOW)
    normed_turned_ref[own_rows:, :] = whole_ref[pl.ds(other_at, own_rows), :].astype(LOW)
    normed = normed.astype(LOW)
    queries = product(normed, query_ref[...]).astype(LOW)
    keys = product(normed, key_ref[...]).astype(LOW)
    values = product(normed, value_ref[...]).astype(LOW)
    qkv_ref[:, 0:columns] = queries
    qkv_ref[:, columns : 2 * columns] = keys
    qkv_ref[:, 2 * columns : 3 * columns] = values
    qkv_ref.send()
    normed_turned_ref.send()
    per_offset = product(
        table_ref[...], wrapped_buckets(buckets, group_rows), 1, 0, HIGHEST
    )
    row_at = lax.broadcasted_iota(jnp.int32, (group_rows, group_rows), 0)
    column_at = lax.broadcasted_iota(jnp.int32, (group_rows, group_rows), 1)
    row_part = jnp.zeros((group_rows, group_rows), jnp.int32)
    column_part = jnp.zeros((group_rows, group_rows), jnp.int32)
    end = 0
    for part in range(lengths_ref.shape[1] - 1):
        end = end + lengths_ref[0, part]
        row_part = row_part + (row_at >= end).astype(jnp.int32)
        column_part = column_part + (column_at >= end).astype(jnp.int32)
    same = row_part == column_part
    mixed_parts = []
    for head in range(heads):
        here = slice(head * head_size, (head + 1) * head_size)
        bias = pltpu.roll(
            jnp.broadcast_to(per_offset[head : head + 1, :], (group_rows, group_rows)),
            0,
            1,
            stride=1,
            stride_axis=0,
        )
        scores = product(queries[:, here], keys[:, here], 1, 1)
        scores = jnp.where(same, scores * scale + bias, EXCLUDED)
        raised = jnp.exp(scores - jnp.max(scores, axis=-1, keepdims=True))
        probs = raised * (1.0 / jnp.sum(raised, axis=-1, keepdims=True))
        probs = probs.astype(LOW)
        probs_ref[head] = probs
        mixed_parts.append(product(probs, values[:, here]))
    probs_ref.send()
    mixed = jnp.concatenate(mixed_parts, axis=1).astype(LOW)
    mixed_ref[...] = mixed
    mixed_ref.send()
    whole_ref[...] = product(mixed, output_ref[...])
    own_ref[...] = whole_ref[pl.ds(own_at, own_rows), :]
    other_ref[...] = whole_ref[pl.ds(other_at, own_rows), :]


def hidden_kernel(
    routes_ref,
    cotangent_ref,
    tokens_ref,
    own_ref,
    gain_ref,
    normed_ref,
    came_ref,
    place_ref,
    hidden_ref,
    sent_ref,
    normed_own_ref,
    *,
    experts,
    capacity,
):
    own_rows, width = own_ref.shape
    slots = place_ref.shape[0]
    place = placed_rows(routes_ref[...], experts, capacity, slots)
    place_ref[...] = place
    place_ref.send()
    sent_ref[:, width:] = product(place, cotangent_ref[...]).astype(LOW)
    own_at = pl.multiple_of(lax.axis_index("shard") * own_rows, own_rows)
    inputs = tokens_ref[pl.ds(own_at, own_rows), :].astype(FULL)
    hidden = inputs + (own_ref[...] + came_ref[...])
    normed = (hidden * inverse_rms(hidden) * gain_ref[...].reshape(1, -1)).astype(LOW)
    sent_ref[:, 0:width] = product(place, normed).astype(LOW)
    sent_ref.send()
    hidden_ref[...] = hidden
    normed_own_ref[...] = normed_ref[0:own_rows, :]


def expert_kernel(
    arrived_ref,
    router_ref,
    in_own_ref,
    out_own_ref,
    in_came_ref,
    out_came_ref,
    back_ref,
    grad_back_ref,
    grad_router_ref,
    rows_ref,
    grad_produced_ref,
    active_own_ref,
    active_came_ref,
    grad_pre_own_ref,
    grad_pre_came_ref,
    *more,
):
    floor_refs, (in_held_ref, out_held_ref, arrived) = more[:-3], more[-3:]
    width, units = in_own_ref.shape
    copies = [
        pltpu.make_async_copy(source, target, arrived.at[at])
        for at, (source, target) in enumerate(
            (
                (in_own_ref, in_held_ref.at[0]),
                (out_own_ref, out_held_ref.at[0]),
                (in_came_ref, in_held_ref.at[1]),
                (out_came_ref, out_held_ref.at[1]),
            )
        )
    ]
    for copy in copies:
        copy.start()
    rows = arrived_ref[:, 0:width]
    grads = arrived_ref[:, width:].astype(FULL)
    rows_ref[...] = rows
    rows_ref.send()
    logits = product(rows, router_ref[...], 1, 1)
    raised = jnp.exp(logits - jnp.max(logits, axis=-1, keepdims=True))
    chances = raised * (1.0 / jnp.sum(raised, axis=-1, keepdims=True))
    chosen = lax.broadcasted_iota(jnp.int32, chances.shape, 1) == lax.axis_index("expert")
    gate = jnp.sum(jnp.where(chosen, chances, 0.0), axis=1, keepdims=True)
    grad_produced = (gate * grads).astype(LOW)
    grad_produced_ref[...] = grad_produced
    grad_produced_ref.send()
    produced = 0.0
    grad_rows = 0.0
    block = 512
    for source in range(2):
        copies[2 * source].wait()
        copies[2 * source + 1].wait()
        active_ref = (active_own_ref, active_came_ref)[source]
        grad_pre_ref = (grad_pre_own_ref, grad_pre_came_ref)[source]
        for first in range(0, units, block):
            here = slice(first, first + block)
            in_block = in_held_ref[source, :, here]
            out_block = out_held_ref[source, here, :]
            pre = product(rows, in_block)
            grad_active = product(grad_produced, out_block, 1, 1)
            steep = 1.0 / (1.0 + 0.2316419 * jnp.abs(pre))
            density = jnp.exp(-0.5 * pre * pre) * 0.3989422804014327
            tail = 1.330274429
            for factor in (-1.821255978, 1.781477937, -0.356563782, 0.319381530):
                tail = tail * steep + factor
            tail = tail * steep * density
            cumulative = jnp.where(pre >= 0.0, 1.0 - tail, tail)
            active = (pre * cumulative).astype(LOW)
            grad_pre = (grad_active * (cumulative + pre * density)).astype(LOW)
            active_ref[:, here] = active
            grad_pre_ref[:, here] = grad_pre
            produced = produced + product(active, out_block)
            grad_rows = grad_rows + product(grad_pre, in_block, 1, 1)
        active_ref.send()
        grad_pre_ref.send()
    produced = produced.astype(LOW).astype(FULL)
    grad_gate = jnp.sum(grads * produced, axis=1, keepdims=True)
    grad_logits = (grad_gate * chances * (chosen.astype(FULL) - gate)).astype(LOW)
    grad_back_ref[...] = (grad_rows + product(grad_logits, router_ref[...])).astype(LOW)
    grad_back_ref.send()
    back_ref[...] = (gate * produced).astype(LOW)
    grad_router_ref[...] = product(grad_logits, rows, 0, 0)
    floor_rows(back_ref, floor_refs)


def halves(own_rows):
    half = lax.axis_index("shard")
    own_at = pl.multiple_of(half * own_rows, own_rows)
    other_at = pl.multiple_of((1 - half) * own_rows, own_rows)
    return (own_at, other_at)


def attention_back_kernel(
    place_own_ref,
    place_came_ref,
    hidden_own_ref,
    hidden_came_ref,
    gain_ref,
    cotangent_own_ref,
    cotangent_came_ref,
    returned_own_ref,
    returned_came_ref,
    output_ref,
    mixed_ref,
    qkv_ref,
    probs_ref,
    attention_ref,
    grad_ffn_ref,
    grad_low_ref,
    grad_table_ref,
    part_ref,
    part_one_ref,
    part_two_ref,
    part_three_ref,
    grads_ref,
    turned_ref,
    output_grad_ref,
    *,
    head_size,
    bucket_total,
):
    own_rows, width = hidden_own_ref.shape
    group_rows = 2 * own_rows
    heads = probs_ref.shape[0]
    columns = heads * head_size
    scale = head_size ** (-0.5)
    own_at, other_at = halves(own_rows)
    gain = gain_ref[...].reshape(1, -1)
    grad_gains = []
    for at, place, rows, cotangent, returned in (
        (own_at, place_own_ref, hidden_own_ref, cotangent_own_ref, returned_own_ref),
        (other_at, place_came_ref, hidden_came_ref, cotangent_came_ref, returned_came_ref),
    ):
        hidden = rows[...]
        grads = product(place[...], returned[...], 0, 0)
        grad_rows, grad_gain = norm_back(hidden, inverse_rms(hidden), gain, grads)
        grad_rows = cotangent[...].astype(FULL) + grad_rows
        attention_ref[pl.ds(at, own_rows), :] = grad_rows.astype(LOW)
        grad_gains.append(grad_gain)
    grad_ffn_ref[...] = grad_gains[0] + grad_gains[1]
    attention_ref.send()
    grad_mixed = product(attention_ref[...], output_ref[...], 1, 1).astype(LOW)
    output_grad_ref[...] = product(mixed_ref[...], attention_ref[...], 0, 0)
    reversal = (
        lax.broadcasted_iota(jnp.int32, (group_rows, group_rows), 0)
        + lax.broadcasted_iota(jnp.int32, (group_rows, group_rows), 1)
        == group_rows - 1
    )
    reversal = reversal.astype(FULL).astype(LOW)
    grad_queries, grad_keys, grad_values, sums = [], [], [], []
    for head in range(heads):
        first = head * head_size
        queries = qkv_ref[:, first : first + head_size]
        keys = qkv_ref[:, columns + first : columns + first + head_size]
        values = qkv_ref[:, 2 * columns + first : 2 * columns + first + head_size]
        probs = probs_ref[head].astype(FULL)
        grad_head = grad_mixed[:, first : first + head_size]
        grad_probs = product(grad_head, values, 1, 1)
        inner = jnp.sum(probs * grad_probs, axis=-1, keepdims=True)
        grad_scores = probs * (grad_probs - inner)
        upper = grad_scores.astype(LOW)
        rest = (grad_scores - upper.astype(FULL)).astype(LOW)
        backwards = product(reversal, upper) + product(reversal, rest)
        aligned = pltpu.roll(backwards, 1, 1, stride=1, stride_axis=0)
        sums.append(jnp.sum(aligned, axis=0, keepdims=True))
        grad_queries.append(product(upper, keys) * scale)
        grad_keys.append(product(upper, queries, 0, 0) * scale)
        grad_values.append(product(probs_ref[head], grad_head, 0, 0))
    grad_table_ref[...] = product(
        jnp.concatenate(sums, axis=0), wrapped_buckets(bucket_total, group_rows), 1, 1, HIGHEST
    )
    grad_queries = jnp.concatenate(grad_queries, axis=1)
    grad_keys = jnp.concatenate(grad_keys, axis=1)
    grad_values = jnp.concatenate(grad_values, axis=1)
    grads_ref[:, 0:columns] = grad_values
    grads_ref[:, columns : 2 * columns] = grad_queries
    grads_ref[:, 2 * columns : 3 * columns] = grad_keys
    grad_low_ref[...] = grads_ref[...].astype(LOW)
    grad_low_ref.send()
    turned_ref[:, 0:own_rows] = grads_ref[pl.ds(own_at, own_rows), :].T
    turned_ref[:, own_rows:] = grads_ref[pl.ds(other_at, own_rows), :].T
    mine = lax.rem(lax.axis_index("expert"), PLANE)
    rows = columns // PLANE
    refs = (part_ref, part_one_ref, part_two_ref, part_three_ref)
    for other, ref in enumerate(refs):
        for weight in range(3):
            at = pl.multiple_of((mine ^ other) * rows + weight * columns, 16)
            ref[weight * rows : (weight + 1) * rows, :] = turned_ref[pl.ds(at, rows), :].astype(
                LOW
            )
        at = pl.multiple_of((mine ^ other) * rows, 16)
        quarter = output_grad_ref[pl.ds(at, rows), :].astype(LOW)
        for piece in range(width // group_rows):
            ref[(3 + piece) * rows : (4 + piece) * rows, :] = quarter[
                :, piece * group_rows : (piece + 1) * group_rows
            ]
        ref.send()


def floor_rows(back_ref, outs):
    rows = outs[0].shape[0]
    for other, ref in enumerate(outs):
        if len(outs) == 1:
            ref[...] = back_ref[...]
        else:
            mine = lax.rem(lax.axis_index("expert") // PLANE, LINE)
            at = pl.multiple_of((mine ^ other) * rows, 16)
            ref[...] = back_ref.ref[pl.ds(at, rows), :]
        ref.send()


def member_rows_kernel(*refs):
    floors, outs = refs[0:LINE], refs[LINE:]
    mine = lax.rem(lax.axis_index("expert"), PLANE)
    rows = outs[0].shape[0] // LINE
    for other, out_ref in enumerate(outs):
        at = pl.multiple_of((mine ^ other) * rows, 16)
        for floor, ref in enumerate(floors):
            ref.ready()
            out_ref[floor * rows : (floor + 1) * rows, :] = ref[pl.ds(at, rows), :]
        out_ref.send()


def returned_rows_kernel(*refs):
    parts, place_ref, hidden_ref, out_ref, done_ref, returned_ref = refs[0:PLANE], *refs[PLANE:]
    member = lax.rem(lax.axis_index("expert"), PLANE)
    floor = lax.rem(lax.axis_index("expert") // PLANE, LINE)
    rows = parts[0].shape[0] // LINE
    for across, ref in enumerate(parts):
        for along in range(LINE):
            at = pl.multiple_of(((floor ^ along) * PLANE + (member ^ across)) * rows, 16)
            returned_ref[pl.ds(at, rows), :] = ref[along * rows : (along + 1) * rows, :]
    out_ref[...] = (
        hidden_ref[...] + product(place_ref[...], returned_ref[...], 0, 0)
    ).astype(LOW)
    done_ref[...] = jnp.zeros(done_ref.shape, FULL)


def grad_tokens_kernel(
    tokens_ref,
    gain_ref,
    attention_ref,
    router_own_ref,
    router_came_ref,
    ffn_ref,
    table_ref,
    grads_own_ref,
    value_own_ref,
    query_own_ref,
    key_own_ref,
    value_came_ref,
    query_came_ref,
    key_came_ref,
    grads_came_ref,
    grad_tokens_ref,
    small_ref,
):
    width, columns = value_own_ref.shape
    experts = router_own_ref.shape[0]
    heads, buckets = table_ref.shape
    sums = []
    for grads, weights in (
        (grads_own_ref, (value_own_ref, query_own_ref, key_own_ref)),
        (grads_came_ref, (value_came_ref, query_came_ref, key_came_ref)),
    ):
        total = 0.0
        for at, ref in enumerate(weights):
            part = grads[:, at * columns : (at + 1) * columns]
            total = total + product(part, ref[...], 1, 1)
        sums.append(total)
    grad_normed = sums[0] + sums[1]
    inputs = tokens_ref[...].astype(FULL)
    grad_rows, grad_gain = norm_back(
        inputs, inverse_rms(inputs), gain_ref[...].reshape(1, -1), grad_normed
    )
    grad_tokens_ref[...] = grad_rows + attention_ref[...].astype(FULL)
    table = jnp.concatenate([table_ref[...], jnp.zeros((heads, width - buckets), FULL)], axis=1)
    early = -(-(experts + 1) // 8) * 8
    small_ref[...] = jnp.concatenate(
        [
            router_own_ref[...] + router_came_ref[...],
            ffn_ref[...],
            jnp.zeros((early - experts - 1, width), FULL),
            grad_gain,
            table,
            jnp.zeros((small_ref.shape[0] - early - heads - 1, width), FULL),
        ],
        axis=0,
    ).astype(small_ref.dtype)


def line_chunks(totals, refs, total_refs, shared=()):
    mine = lax.rem(lax.axis_index("expert") // PLANE, LINE)
    for total, total_ref in zip(totals, total_refs):
        total_ref[...] = total
    for other, ref in enumerate(refs):
        chunks = []
        for total_ref in total_refs:
            rows = total_ref.shape[0] // LINE
            at = pl.multiple_of((mine ^ other) * rows, 8)
            chunks.append(total_ref[pl.ds(at, rows), :])
        ref[...] = jnp.concatenate(chunks + list(shared), axis=0).astype(ref.dtype)
        ref.send()


def sums_kernel(*refs):
    parts, nears, fars, normed_ref, small_ref = refs[0:4], refs[4:7], refs[7:10], *refs[10:12]
    outs, total_refs = refs[12:16], refs[16:20]
    own_rows = normed_ref.shape[0] // 2
    rows = total_refs[0].shape[0]
    pieces = normed_ref.shape[1] // parts[0].shape[1]
    output = 0.0
    weights = 0.0
    for at, part in enumerate(parts):
        output = output + jnp.concatenate(
            [part[(3 + piece) * rows : (4 + piece) * rows, :] for piece in range(pieces)], axis=1
        ).astype(FULL)
        near = nears[at - 1][...] if at else normed_ref[0:own_rows]
        far = fars[at - 1][...] if at else normed_ref[own_rows:]
        weights = weights + product(part[0 : 3 * rows, 0:own_rows], near)
        weights = weights + product(part[0 : 3 * rows, own_rows:], far)
    totals = (weights[0:rows], weights[rows : 2 * rows], weights[2 * rows :], output)
    line_chunks(totals, outs, total_refs, (small_ref[...].astype(FULL),))


def summed(refs, rows=slice(None)):
    near = refs[0][rows, :].astype(FULL) + refs[1][rows, :].astype(FULL)
    far = refs[2][rows, :].astype(FULL) + refs[3][rows, :].astype(FULL)
    return near + far


def line_sum_kernel(*refs):
    total = summed(refs[0:LINE])
    for out_ref in refs[LINE:]:
        out_ref[...] = total[0 : out_ref.shape[0]].astype(out_ref.dtype)


def assemble_kernel(*refs):
    chunk_refs = refs[0 : PLANE * LINE]
    value_ref, query_ref, key_ref, output_ref, router_ref, ffn_ref, attn_ref, table_ref = refs[
        PLANE * LINE : -3
    ]
    totals = refs[-3:] + (output_ref.ref,)
    member = lax.rem(lax.axis_index("expert"), PLANE)
    floor = lax.rem(lax.axis_index("expert") // PLANE, LINE)
    rows = output_ref.shape[0] // PLANE // LINE
    for along in range(LINE):
        for across in range(PLANE):
            chunk = chunk_refs[along * PLANE + across][0 : 4 * rows, :].astype(FULL)
            at = pl.multiple_of(((member ^ across) * LINE + (floor ^ along)) * rows, 8)
            for weight, total_ref in enumerate(totals):
                total_ref[pl.ds(at, rows), :] = chunk[weight * rows : (weight + 1) * rows]
    output_ref.send()
    for total_ref, ref in zip(totals, (value_ref, query_ref, key_ref)):
        ref[...] = total_ref[...].T
        ref.send()
    small = summed(chunk_refs[0:PLANE], slice(4 * rows, None))
    experts = router_ref.shape[0]
    heads, buckets = table_ref.shape
    late = -(-(experts + 1) // 8) * 8
    router_ref[...] = small[0:experts]
    ffn_ref[...] = small[experts : experts + 1].reshape(-1)
    attn_ref[...] = small[late : late + 1].reshape(-1)
    table_ref[...] = small[late + 1 : late + 1 + heads, 0:buckets]


def expert_grads_kernel(
    rows_ref,
    rows_far_ref,
    grad_produced_ref,
    grad_produced_far_ref,
    active_ref,
    active_far_ref,
    grad_pre_ref,
    grad_pre_far_ref,
    grad_in_ref,
    grad_out_ref,
    done_ref,
):
    done_ref[...] = jnp.zeros_like(done_ref)
    grad_in_ref[...] = product(rows_ref[...], grad_pre_ref[...], 0, 0) + product(
        rows_far_ref[...], grad_pre_far_ref[...], 0, 0
    )
    grad_out_ref[...] = product(active_ref[...], grad_produced_ref[...], 0, 0) + product(
        active_far_ref[...], grad_produced_far_ref[...], 0, 0
    )


def expert_grads(rows, rows_far, grad_produced, grad_produced_far, *wide):
    slots, width = rows.shape
    units = wide[0].shape[1]
    block = 768
    fixed = pl.BlockSpec((slots, width), lambda step: (0, 0))
    moving = pl.BlockSpec((slots, block), lambda step: (0, step))
    return pl.pallas_call(
        expert_grads_kernel,
        grid=(units // block,),
        out_shape=[
            jax.ShapeDtypeStruct((width, units), FULL),
            jax.ShapeDtypeStruct((units, width), FULL),
            jax.ShapeDtypeStruct((8, 128), FULL),
        ],
        in_specs=[fixed] * 4 + [moving] * 4,
        out_specs=[
            pl.BlockSpec((width, block), lambda step: (0, step)),
            pl.BlockSpec((block, width), lambda step: (step, 0)),
            pl.BlockSpec((8, 128), lambda step: (0, 0)),
        ],
        compiler_params=pltpu.CompilerParams(vmem_limit_bytes=56 * MEGABYTE),
        cost_estimate=pl.CostEstimate(flops=0, bytes_accessed=0, transcendentals=0),
    )(rows, rows_far, grad_produced, grad_produced_far, *wide)


def block_out_kernel(place_ref, returned_ref, hidden_ref, out_ref):
    out_ref[...] = (
        hidden_ref[...] + product(place_ref[...], returned_ref[...], 0, 0)
    ).astype(LOW)


def shards(
    tokens,
    attn_gain,
    query_weight,
    key_weight,
    value_weight,
    output_weight,
    bias_table,
    ffn_gain,
    router_weight,
    expert_in,
    expert_out,
    routes,
    lengths,
    cotangent,
):
    group_rows, width = tokens.shape
    own_rows = cotangent.shape[0]
    heads = bias_table.shape[1]
    buckets = bias_table.shape[0]
    columns = query_weight.shape[1]
    head_size = columns // heads
    sources = lax.axis_size("expert")
    experts = router_weight.shape[1]
    capacity = 2 * own_rows // experts
    slots = experts * capacity
    beyond = sources // (PLANE * LINE)
    router_rows = router_weight.T

    def swap(item):
        return lax.ppermute(item, "shard", [(0, 1), (1, 0)])

    def hop(item, distance):
        return lax.ppermute(item, "expert", [(at, at ^ distance) for at in range(sources)])

    def around(items, stride):
        return tuple(hop(item, stride * (step + 1)) for step, item in enumerate(items))

    def exchange(rows):
        parts = rows.reshape(sources, slots // sources, rows.shape[1])
        came = lax.all_to_all(parts, "expert", split_axis=0, concat_axis=0, tiled=True)
        return came.reshape(rows.shape)

    def beyond_sum(item):
        if beyond == 1:
            return item
        groups = [
            [near + PLANE * LINE * far for far in range(beyond)] for near in range(PLANE * LINE)
        ]
        return lax.psum(item, "expert", axis_index_groups=groups)

    in_own, out_own = expert_in[0], expert_out[0]
    in_came, out_came = swap(in_own), swap(out_own)
    own, other, qkv, probs, normed, mixed = run(
        functools.partial(forward_kernel, head_size=head_size),
        [
            ((own_rows, width), FULL),
            ((own_rows, width), FULL),
            ((group_rows, 3 * columns), LOW),
            ((heads, group_rows, group_rows), LOW),
            ((group_rows, width), LOW),
            ((group_rows, columns), LOW),
        ],
        (
            lengths,
            tokens,
            attn_gain,
            query_weight,
            key_weight,
            value_weight,
            bias_table.T,
            output_weight,
        ),
        scratch=(pltpu.VMEM((group_rows, width), FULL),),
        scalars=1,
    )
    place, hidden, sent, normed_own = run(
        functools.partial(hidden_kernel, experts=experts, capacity=capacity),
        [
            ((slots, own_rows), LOW),
            ((own_rows, width), FULL),
            ((slots, 2 * width), LOW),
            ((own_rows, width), LOW),
        ],
        (routes.reshape(1, own_rows), cotangent, tokens, own, ffn_gain, normed, swap(other)),
    )
    normed_near = around((normed_own,) * 3, 1)
    floors = LINE if beyond == 1 else 1
    (
        back,
        grad_back,
        grad_router,
        rows,
        grad_produced,
        active_own,
        active_came,
        grad_pre_own,
        grad_pre_came,
        *floor_back,
    ) = run(
        expert_kernel,
        [
            ((slots, width), LOW),
            ((slots, width), LOW),
            ((experts, width), FULL),
            ((slots, width), LOW),
            ((slots, width), LOW),
        ]
        + [((slots, in_own.shape[1]), LOW)] * 4
        + [((slots // floors, width), LOW)] * floors,
        (exchange(sent), router_rows, in_own, out_own, in_came, out_came),
        scratch=(
            pltpu.VMEM((2, *in_own.shape), LOW),
            pltpu.VMEM((2, *out_own.shape), LOW),
            pltpu.SemaphoreType.DMA((4,)),
        ),
        raw=(2, 3, 4, 5),
        after=normed_near,
    )
    returned_grads = exchange(grad_back)
    rows_far, grad_produced_far = swap(rows), swap(grad_produced)
    active_far, grad_pre_far = swap(active_came), swap(grad_pre_came)
    grad_router_came = swap(grad_router)
    place_came, hidden_came, cotangent_came = swap(place), swap(hidden), swap(cotangent)
    small_rows = -(-(experts + 1) // 8) * 8
    part_rows = columns // PLANE
    attention, grad_ffn, grads_low, grad_table, *parts = run(
        functools.partial(attention_back_kernel, head_size=head_size, bucket_total=buckets),
        [
            ((group_rows, width), LOW),
            ((1, width), FULL),
            ((group_rows, 3 * columns), LOW),
            ((heads, buckets), FULL),
        ]
        + [((part_rows * (3 + width // group_rows), group_rows), LOW)] * PLANE,
        (
            place,
            place_came,
            hidden,
            hidden_came,
            ffn_gain,
            cotangent,
            cotangent_came,
            returned_grads,
            swap(returned_grads),
            output_weight,
            mixed,
            qkv,
            probs,
        ),
        scratch=(
            pltpu.VMEM((group_rows, 3 * columns), FULL),
            pltpu.VMEM((3 * columns, group_rows), FULL),
            pltpu.VMEM((columns, width), FULL),
        ),
        after=(
            rows_far,
            grad_produced_far,
            active_far,
            grad_pre_far,
            grad_router_came,
        ),
    )
    parts = (parts[0],) + around(parts[1:], 1)
    grads_came = swap(grads_low)
    weights = (value_weight, query_weight, key_weight)
    weights_came = tuple(swap(item) for item in weights)
    normed_far = tuple(swap(item) for item in normed_near)
    late_rows = -(-(heads + 1) // 8) * 8
    grad_tokens, small = run(
        grad_tokens_kernel,
        [
            ((group_rows, width), FULL),
            ((small_rows + late_rows, width), LOW),
        ],
        (
            tokens,
            attn_gain,
            attention,
            grad_router,
            grad_router_came,
            grad_ffn,
            grad_table,
            grads_low,
            *weights,
            *weights_came,
            grads_came,
        ),
    )
    if beyond == 1:
        floor_back = (floor_back[0],) + around(floor_back[1:], PLANE)
    chunk_rows = 4 * part_rows // LINE
    all_rows = chunk_rows + small_rows + late_rows
    chunks = run(
        sums_kernel,
        [((all_rows, width), LOW)] * LINE,
        parts + normed_near + normed_far + (normed, small),
        scratch=(pltpu.VMEM((part_rows, width), FULL),) * 4,
        after=tuple(floor_back[1:]),
    )
    chunks = (chunks[0],) + around(chunks[1:], PLANE)
    grad_expert_in, grad_expert_out, done = expert_grads(
        rows,
        rows_far,
        grad_produced,
        grad_produced_far,
        active_own,
        active_far,
        grad_pre_own,
        grad_pre_far,
    )
    if beyond == 1:
        back = run(
            member_rows_kernel, [((slots // PLANE, width), LOW)] * PLANE, floor_back, after=(chunks[1],)
        )
        back = (back[0],) + around(back[1:], 1)
        block_out, returned_done = run(
            returned_rows_kernel,
            [((own_rows, width), LOW), ((8, 128), FULL)],
            tuple(back) + (place, hidden),
            scratch=(pltpu.VMEM((slots, width), LOW),),
        )
    else:
        (block_out,) = run(
            block_out_kernel, [((own_rows, width), LOW)], (place, exchange(back), hidden)
        )
    if beyond == 1:
        whole, chunk = run(
            line_sum_kernel,
            [((all_rows, width), LOW), ((chunk_rows, width), LOW)],
            chunks,
            near=True,
            after=(done,),
        )
    else:
        (whole,) = run(line_sum_kernel, [((all_rows, width), FULL)], chunks)
        whole = beyond_sum(whole).astype(LOW)
        chunk = whole[0:chunk_rows]
    gathered = (whole,) + around((whole,) * 3, 1)
    opposite = gathered[PLANE - 1]
    for along, item in enumerate(around((chunk,) * 3, PLANE)):
        near_two = around((item,) * 2, 1)
        if along < 2:
            third = hop(opposite, PLANE * (along + 1))
        else:
            third = hop(item, PLANE - 1)
        gathered += (item,) + near_two + (third,)
    (
        grad_value,
        grad_query,
        grad_key,
        grad_output,
        grad_router,
        grad_ffn_gain,
        grad_attn_gain,
        grad_table,
    ) = run(
        assemble_kernel,
        [((width, columns), FULL)] * 3
        + [((columns, width), FULL), ((experts, width), FULL), ((width,), FULL), ((width,), FULL)]
        + [((heads, buckets), FULL)],
        gathered,
        scratch=(pltpu.VMEM((columns, width), FULL),) * 3,
        after=(block_out,),
    )
    grad_router = grad_router.T
    grad_table = grad_table.T
    return (
        block_out,
        grad_tokens,
        grad_attn_gain,
        grad_query,
        grad_key,
        grad_value,
        grad_output,
        grad_table,
        grad_ffn_gain,
        grad_router,
        grad_expert_in[None],
        grad_expert_out[None],
    )


def solution(mesh):
    return jax.shard_map(
        shards,
        mesh=mesh,
        in_specs=(
            P("expert", None),
            P(),
            P(None, "shard"),
            P(None, "shard"),
            P(None, "shard"),
            P("shard", None),
            P(None, "shard"),
            P(),
            P(),
            P("expert", None, "shard"),
            P("expert", "shard", None),
            P(("expert", "shard"), None),
            P("expert", None),
            P(("expert", "shard"), None),
        ),
        out_specs=(
            P(("expert", "shard"), None),
            P("expert", None),
            P(),
            P(None, "shard"),
            P(None, "shard"),
            P(None, "shard"),
            P("shard", None),
            P(None, "shard"),
            P(),
            P(),
            P("expert", None, "shard"),
            P("expert", "shard", None),
        ),
        check_vma=False,
    )
```

```python
import functools

import jax
import jax.numpy as jnp
from jax import lax
from jax.experimental import pallas as pl
from jax.experimental.pallas import tpu as pltpu
from jax.sharding import PartitionSpec as P

EPSILON = 1e-06
BORDERS = (12, 16, 23, 32, 46, 64, 91)
HIGHEST = lax.Precision.HIGHEST
EXCLUDED = -1e30
PLANE = 4
LINE = 4
LOW = jnp.bfloat16
FULL = jnp.float32
MEGABYTE = 1024 * 1024


def inverse_rms(rows):
    return lax.rsqrt(jnp.mean(rows * rows, axis=-1, keepdims=True) + EPSILON)


def norm_back(rows, scale_rows, gain, grad_normed):
    scaled = grad_normed * gain
    grad_rows = scale_rows * scaled - rows * scale_rows**3 * jnp.mean(
        scaled * rows, axis=-1, keepdims=True
    )
    grad_gain = jnp.sum(grad_normed * rows * scale_rows, axis=0, keepdims=True)
    return (grad_rows, grad_gain)


def product(left, right, left_dim=1, right_dim=0, precision=None):
    return lax.dot_general(
        left,
        right,
        (((left_dim,), (right_dim,)), ((), ())),
        precision=precision,
        preferred_element_type=FULL,
    )


def wrapped_buckets(bucket_total, columns):
    column = lax.broadcasted_iota(jnp.int32, (bucket_total, columns), 1)
    offset = jnp.where(column < columns // 2, column, column - columns)
    magnitude = jnp.abs(offset)
    bucket = jnp.minimum(magnitude, 8)
    for border in BORDERS:
        bucket = bucket + (magnitude >= border).astype(jnp.int32)
    bucket = bucket + 16 * (offset > 0).astype(jnp.int32)
    rows = lax.broadcasted_iota(jnp.int32, (bucket_total, columns), 0)
    return (bucket == rows).astype(FULL)


class Fetched:
    def __init__(self, ref, copy):
        self.ref = ref
        self.copy = copy
        self.shape = ref.shape

    def ready(self):
        if self.copy is not None:
            self.copy.wait()
            self.copy = None

    def __getitem__(self, index):
        self.ready()
        return self.ref[index]


class Sent:
    def __init__(self, ref, copy):
        self.ref = ref
        self.copy = copy
        self.shape = ref.shape
        self.dtype = ref.dtype
        self.started = False

    def __getitem__(self, index):
        return self.ref[index]

    def __setitem__(self, index, value):
        self.ref[index] = value

    def send(self):
        if not self.started:
            self.copy.start()
            self.started = True


def run(kernel, outs, operands, scratch=(), scalars=0, raw=(), after=(), near=False, grant=56):
    count, results = len(operands), len(outs)
    brought = [] if near else [at for at in range(scalars, count) if at not in raw]

    def body(*refs):
        refs = list(refs)
        given = refs[:count]
        rest = refs[count + len(after) :]
        targets, rest = rest[:results], rest[results:]
        if near:
            kernel(*given, *targets, *rest)
            return
        own, rest = rest[: len(scratch)], rest[len(scratch) :]
        buffers, rest = rest[: len(brought)], rest[len(brought) :]
        built, (arrived, left) = rest[:results], rest[results:]
        for slot, (at, buffer) in enumerate(zip(brought, buffers)):
            copy = pltpu.make_async_copy(given[at], buffer, arrived.at[slot])
            copy.start()
            given[at] = Fetched(buffer, copy)
        sent = [
            Sent(buffer, pltpu.make_async_copy(buffer, target, left.at[slot]))
            for slot, (buffer, target) in enumerate(zip(built, targets))
        ]
        kernel(*given, *sent, *own)
        for at in brought:
            given[at].ready()
        for item in sent:
            item.send()
        for item in sent:
            item.copy.wait()

    anywhere = pl.BlockSpec(memory_space=pl.ANY)
    placed = pl.BlockSpec(memory_space=pltpu.VMEM) if near else anywhere
    in_specs = [pl.BlockSpec(memory_space=pltpu.SMEM)] * scalars
    in_specs += [placed] * (count - scalars) + [anywhere] * len(after)
    scratch_shapes = list(scratch)
    if not near:
        scratch_shapes += [pltpu.VMEM(operands[at].shape, operands[at].dtype) for at in brought]
        scratch_shapes += [pltpu.VMEM(shape, dtype) for shape, dtype in outs]
        scratch_shapes += [pltpu.SemaphoreType.DMA((len(brought),))]
        scratch_shapes += [pltpu.SemaphoreType.DMA((results,))]
    return pl.pallas_call(
        body,
        out_shape=[jax.ShapeDtypeStruct(shape, dtype) for shape, dtype in outs],
        in_specs=in_specs,
        out_specs=[placed] * results,
        scratch_shapes=scratch_shapes,
        compiler_params=pltpu.CompilerParams(vmem_limit_bytes=(4 if near else grant) * MEGABYTE),
        cost_estimate=pl.CostEstimate(flops=0, bytes_accessed=0, transcendentals=0),
    )(*operands, *after)


def placed_rows(chosen, experts, capacity, slots):
    own_rows = chosen.shape[1]
    picked = chosen == lax.broadcasted_iota(jnp.int32, (experts, own_rows), 0)
    picked_float = picked.astype(FULL)
    earlier = lax.broadcasted_iota(jnp.int32, (own_rows, own_rows), 0) < lax.broadcasted_iota(
        jnp.int32, (own_rows, own_rows), 1
    )
    ranks = product(picked_float.astype(LOW), earlier.astype(FULL).astype(LOW))
    rank = jnp.sum(ranks * picked_float, axis=0, keepdims=True)
    target = chosen * capacity + rank.astype(jnp.int32)
    place = target == lax.broadcasted_iota(jnp.int32, (slots, own_rows), 0)
    return place.astype(FULL).astype(LOW)


def forward_kernel(
    lengths_ref,
    tokens_ref,
    gain_ref,
    query_ref,
    key_ref,
    value_ref,
    table_ref,
    output_ref,
    own_ref,
    other_ref,
    qkv_ref,
    probs_ref,
    normed_turned_ref,
    mixed_ref,
    whole_ref,
    *,
    head_size,
):
    group_rows = tokens_ref.shape[0]
    own_rows = own_ref.shape[0]
    heads, buckets = table_ref.shape
    columns = heads * head_size
    scale = head_size ** (-0.5)
    half = lax.axis_index("shard")
    own_at = pl.multiple_of(half * own_rows, own_rows)
    other_at = pl.multiple_of((1 - half) * own_rows, own_rows)
    inputs = tokens_ref[...].astype(FULL)
    normed = inputs * inverse_rms(inputs) * gain_ref[...].reshape(1, -1)
    whole_ref[...] = normed
    normed_turned_ref[0:own_rows, :] = whole_ref[pl.ds(own_at, own_rows), :].astype(LOW)
    normed_turned_ref[own_rows:, :] = whole_ref[pl.ds(other_at, own_rows), :].astype(LOW)
    normed = normed.astype(LOW)
    queries = product(normed, query_ref[...]).astype(LOW)
    keys = product(normed, key_ref[...]).astype(LOW)
    values = product(normed, value_ref[...]).astype(LOW)
    qkv_ref[:, 0:columns] = queries
    qkv_ref[:, columns : 2 * columns] = keys
    qkv_ref[:, 2 * columns : 3 * columns] = values
    qkv_ref.send()
    normed_turned_ref.send()
    per_offset = product(
        table_ref[...], wrapped_buckets(buckets, group_rows), 1, 0, HIGHEST
    )
    row_at = lax.broadcasted_iota(jnp.int32, (group_rows, group_rows), 0)
    column_at = lax.broadcasted_iota(jnp.int32, (group_rows, group_rows), 1)
    row_part = jnp.zeros((group_rows, group_rows), jnp.int32)
    column_part = jnp.zeros((group_rows, group_rows), jnp.int32)
    end = 0
    for part in range(lengths_ref.shape[1] - 1):
        end = end + lengths_ref[0, part]
        row_part = row_part + (row_at >= end).astype(jnp.int32)
        column_part = column_part + (column_at >= end).astype(jnp.int32)
    same = row_part == column_part
    mixed_parts = []
    for head in range(heads):
        here = slice(head * head_size, (head + 1) * head_size)
        bias = pltpu.roll(
            jnp.broadcast_to(per_offset[head : head + 1, :], (group_rows, group_rows)),
            0,
            1,
            stride=1,
            stride_axis=0,
        )
        scores = product(queries[:, here], keys[:, here], 1, 1)
        scores = jnp.where(same, scores * scale + bias, EXCLUDED)
        raised = jnp.exp(scores - jnp.max(scores, axis=-1, keepdims=True))
        probs = raised * (1.0 / jnp.sum(raised, axis=-1, keepdims=True))
        probs = probs.astype(LOW)
        probs_ref[head] = probs
        mixed_parts.append(product(probs, values[:, here]))
    probs_ref.send()
    mixed = jnp.concatenate(mixed_parts, axis=1).astype(LOW)
    mixed_ref[...] = mixed
    mixed_ref.send()
    whole_ref[...] = product(mixed, output_ref[...])
    own_ref[...] = whole_ref[pl.ds(own_at, own_rows), :]
    other_ref[...] = whole_ref[pl.ds(other_at, own_rows), :]


def hidden_kernel(
    routes_ref,
    cotangent_ref,
    tokens_ref,
    own_ref,
    gain_ref,
    normed_ref,
    came_ref,
    place_ref,
    hidden_ref,
    sent_ref,
    normed_own_ref,
    *,
    experts,
    capacity,
):
    own_rows, width = own_ref.shape
    slots = place_ref.shape[0]
    place = placed_rows(routes_ref[...], experts, capacity, slots)
    place_ref[...] = place
    place_ref.send()
    sent_ref[:, width:] = product(place, cotangent_ref[...]).astype(LOW)
    own_at = pl.multiple_of(lax.axis_index("shard") * own_rows, own_rows)
    inputs = tokens_ref[pl.ds(own_at, own_rows), :].astype(FULL)
    hidden = inputs + (own_ref[...] + came_ref[...])
    normed = (hidden * inverse_rms(hidden) * gain_ref[...].reshape(1, -1)).astype(LOW)
    sent_ref[:, 0:width] = product(place, normed).astype(LOW)
    sent_ref.send()
    hidden_ref[...] = hidden
    normed_own_ref[...] = normed_ref[0:own_rows, :]


def expert_kernel(
    arrived_ref,
    router_ref,
    in_own_ref,
    out_own_ref,
    in_came_ref,
    out_came_ref,
    back_ref,
    grad_back_ref,
    grad_router_ref,
    rows_ref,
    grad_produced_ref,
    active_own_ref,
    active_came_ref,
    grad_pre_own_ref,
    grad_pre_came_ref,
    *more,
):
    floor_refs, (in_held_ref, out_held_ref, arrived) = more[:-3], more[-3:]
    width, units = in_own_ref.shape
    copies = [
        pltpu.make_async_copy(source, target, arrived.at[at])
        for at, (source, target) in enumerate(
            (
                (in_own_ref, in_held_ref.at[0]),
                (out_own_ref, out_held_ref.at[0]),
                (in_came_ref, in_held_ref.at[1]),
                (out_came_ref, out_held_ref.at[1]),
            )
        )
    ]
    for copy in copies:
        copy.start()
    rows = arrived_ref[:, 0:width]
    grads = arrived_ref[:, width:].astype(FULL)
    rows_ref[...] = rows
    rows_ref.send()
    logits = product(rows, router_ref[...], 1, 1)
    raised = jnp.exp(logits - jnp.max(logits, axis=-1, keepdims=True))
    chances = raised * (1.0 / jnp.sum(raised, axis=-1, keepdims=True))
    chosen = lax.broadcasted_iota(jnp.int32, chances.shape, 1) == lax.axis_index("expert")
    gate = jnp.sum(jnp.where(chosen, chances, 0.0), axis=1, keepdims=True)
    grad_produced = (gate * grads).astype(LOW)
    grad_produced_ref[...] = grad_produced
    grad_produced_ref.send()
    produced = 0.0
    grad_rows = 0.0
    block = 512
    for source in range(2):
        copies[2 * source].wait()
        copies[2 * source + 1].wait()
        active_ref = (active_own_ref, active_came_ref)[source]
        grad_pre_ref = (grad_pre_own_ref, grad_pre_came_ref)[source]
        for first in range(0, units, block):
            here = slice(first, first + block)
            in_block = in_held_ref[source, :, here]
            out_block = out_held_ref[source, here, :]
            pre = product(rows, in_block)
            grad_active = product(grad_produced, out_block, 1, 1)
            steep = 1.0 / (1.0 + 0.2316419 * jnp.abs(pre))
            density = jnp.exp(-0.5 * pre * pre) * 0.3989422804014327
            tail = 1.330274429
            for factor in (-1.821255978, 1.781477937, -0.356563782, 0.319381530):
                tail = tail * steep + factor
            tail = tail * steep * density
            cumulative = jnp.where(pre >= 0.0, 1.0 - tail, tail)
            active = (pre * cumulative).astype(LOW)
            grad_pre = (grad_active * (cumulative + pre * density)).astype(LOW)
            active_ref[:, here] = active
            grad_pre_ref[:, here] = grad_pre
            produced = produced + product(active, out_block)
            grad_rows = grad_rows + product(grad_pre, in_block, 1, 1)
        active_ref.send()
        grad_pre_ref.send()
    produced = produced.astype(LOW).astype(FULL)
    grad_gate = jnp.sum(grads * produced, axis=1, keepdims=True)
    grad_logits = (grad_gate * chances * (chosen.astype(FULL) - gate)).astype(LOW)
    grad_back_ref[...] = (grad_rows + product(grad_logits, router_ref[...])).astype(LOW)
    grad_back_ref.send()
    back_ref[...] = (gate * produced).astype(LOW)
    grad_router_ref[...] = product(grad_logits, rows, 0, 0)
    floor_rows(back_ref, floor_refs)


def halves(own_rows):
    half = lax.axis_index("shard")
    own_at = pl.multiple_of(half * own_rows, own_rows)
    other_at = pl.multiple_of((1 - half) * own_rows, own_rows)
    return (own_at, other_at)


def attention_back_kernel(
    place_own_ref,
    place_came_ref,
    hidden_own_ref,
    hidden_came_ref,
    gain_ref,
    cotangent_own_ref,
    cotangent_came_ref,
    returned_own_ref,
    returned_came_ref,
    output_ref,
    mixed_ref,
    qkv_ref,
    probs_ref,
    attention_ref,
    grad_ffn_ref,
    grad_low_ref,
    grad_table_ref,
    part_ref,
    part_one_ref,
    part_two_ref,
    part_three_ref,
    grads_ref,
    turned_ref,
    output_grad_ref,
    *,
    head_size,
    bucket_total,
):
    own_rows, width = hidden_own_ref.shape
    group_rows = 2 * own_rows
    heads = probs_ref.shape[0]
    columns = heads * head_size
    scale = head_size ** (-0.5)
    own_at, other_at = halves(own_rows)
    gain = gain_ref[...].reshape(1, -1)
    grad_gains = []
    for at, place, rows, cotangent, returned in (
        (own_at, place_own_ref, hidden_own_ref, cotangent_own_ref, returned_own_ref),
        (other_at, place_came_ref, hidden_came_ref, cotangent_came_ref, returned_came_ref),
    ):
        hidden = rows[...]
        grads = product(place[...], returned[...], 0, 0)
        grad_rows, grad_gain = norm_back(hidden, inverse_rms(hidden), gain, grads)
        grad_rows = cotangent[...].astype(FULL) + grad_rows
        attention_ref[pl.ds(at, own_rows), :] = grad_rows.astype(LOW)
        grad_gains.append(grad_gain)
    grad_ffn_ref[...] = grad_gains[0] + grad_gains[1]
    attention_ref.send()
    grad_mixed = product(attention_ref[...], output_ref[...], 1, 1).astype(LOW)
    output_grad_ref[...] = product(mixed_ref[...], attention_ref[...], 0, 0)
    reversal = (
        lax.broadcasted_iota(jnp.int32, (group_rows, group_rows), 0)
        + lax.broadcasted_iota(jnp.int32, (group_rows, group_rows), 1)
        == group_rows - 1
    )
    reversal = reversal.astype(FULL).astype(LOW)
    grad_queries, grad_keys, grad_values, sums = [], [], [], []
    for head in range(heads):
        first = head * head_size
        queries = qkv_ref[:, first : first + head_size]
        keys = qkv_ref[:, columns + first : columns + first + head_size]
        values = qkv_ref[:, 2 * columns + first : 2 * columns + first + head_size]
        probs = probs_ref[head].astype(FULL)
        grad_head = grad_mixed[:, first : first + head_size]
        grad_probs = product(grad_head, values, 1, 1)
        inner = jnp.sum(probs * grad_probs, axis=-1, keepdims=True)
        grad_scores = probs * (grad_probs - inner)
        upper = grad_scores.astype(LOW)
        rest = (grad_scores - upper.astype(FULL)).astype(LOW)
        backwards = product(reversal, upper) + product(reversal, rest)
        aligned = pltpu.roll(backwards, 1, 1, stride=1, stride_axis=0)
        sums.append(jnp.sum(aligned, axis=0, keepdims=True))
        grad_queries.append(product(upper, keys) * scale)
        grad_keys.append(product(upper, queries, 0, 0) * scale)
        grad_values.append(product(probs_ref[head], grad_head, 0, 0))
    grad_table_ref[...] = product(
        jnp.concatenate(sums, axis=0), wrapped_buckets(bucket_total, group_rows), 1, 1, HIGHEST
    )
    grad_queries = jnp.concatenate(grad_queries, axis=1)
    grad_keys = jnp.concatenate(grad_keys, axis=1)
    grad_values = jnp.concatenate(grad_values, axis=1)
    grads_ref[:, 0:columns] = grad_values
    grads_ref[:, columns : 2 * columns] = grad_queries
    grads_ref[:, 2 * columns : 3 * columns] = grad_keys
    grad_low_ref[...] = grads_ref[...].astype(LOW)
    grad_low_ref.send()
    turned_ref[:, 0:own_rows] = grads_ref[pl.ds(own_at, own_rows), :].T
    turned_ref[:, own_rows:] = grads_ref[pl.ds(other_at, own_rows), :].T
    mine = lax.rem(lax.axis_index("expert"), PLANE)
    rows = columns // PLANE
    refs = (part_ref, part_one_ref, part_two_ref, part_three_ref)
    for other, ref in enumerate(refs):
        for weight in range(3):
            at = pl.multiple_of((mine ^ other) * rows + weight * columns, 16)
            ref[weight * rows : (weight + 1) * rows, :] = turned_ref[pl.ds(at, rows), :].astype(
                LOW
            )
        at = pl.multiple_of((mine ^ other) * rows, 16)
        quarter = output_grad_ref[pl.ds(at, rows), :].astype(LOW)
        for piece in range(width // group_rows):
            ref[(3 + piece) * rows : (4 + piece) * rows, :] = quarter[
                :, piece * group_rows : (piece + 1) * group_rows
            ]
        ref.send()


def floor_rows(back_ref, outs):
    rows = outs[0].shape[0]
    for other, ref in enumerate(outs):
        if len(outs) == 1:
            ref[...] = back_ref[...]
        else:
            mine = lax.rem(lax.axis_index("expert") // PLANE, LINE)
            at = pl.multiple_of((mine ^ other) * rows, 16)
            ref[...] = back_ref.ref[pl.ds(at, rows), :]
        ref.send()


def member_rows_kernel(*refs):
    floors, outs = refs[0:LINE], refs[LINE:]
    mine = lax.rem(lax.axis_index("expert"), PLANE)
    rows = outs[0].shape[0] // LINE
    for other, out_ref in enumerate(outs):
        at = pl.multiple_of((mine ^ other) * rows, 16)
        for floor, ref in enumerate(floors):
            ref.ready()
            out_ref[floor * rows : (floor + 1) * rows, :] = ref[pl.ds(at, rows), :]
        out_ref.send()


def returned_rows_kernel(*refs):
    parts, place_ref, hidden_ref, out_ref, done_ref, returned_ref = refs[0:PLANE], *refs[PLANE:]
    member = lax.rem(lax.axis_index("expert"), PLANE)
    floor = lax.rem(lax.axis_index("expert") // PLANE, LINE)
    rows = parts[0].shape[0] // LINE
    for across, ref in enumerate(parts):
        for along in range(LINE):
            at = pl.multiple_of(((floor ^ along) * PLANE + (member ^ across)) * rows, 16)
            returned_ref[pl.ds(at, rows), :] = ref[along * rows : (along + 1) * rows, :]
    out_ref[...] = (
        hidden_ref[...] + product(place_ref[...], returned_ref[...], 0, 0)
    ).astype(LOW)
    done_ref[...] = jnp.zeros(done_ref.shape, FULL)


def grad_tokens_kernel(
    tokens_ref,
    gain_ref,
    attention_ref,
    router_own_ref,
    router_came_ref,
    ffn_ref,
    table_ref,
    grads_own_ref,
    value_own_ref,
    query_own_ref,
    key_own_ref,
    value_came_ref,
    query_came_ref,
    key_came_ref,
    grads_came_ref,
    grad_tokens_ref,
    small_ref,
):
    width, columns = value_own_ref.shape
    experts = router_own_ref.shape[0]
    heads, buckets = table_ref.shape
    sums = []
    for grads, weights in (
        (grads_own_ref, (value_own_ref, query_own_ref, key_own_ref)),
        (grads_came_ref, (value_came_ref, query_came_ref, key_came_ref)),
    ):
        total = 0.0
        for at, ref in enumerate(weights):
            part = grads[:, at * columns : (at + 1) * columns]
            total = total + product(part, ref[...], 1, 1)
        sums.append(total)
    grad_normed = sums[0] + sums[1]
    inputs = tokens_ref[...].astype(FULL)
    grad_rows, grad_gain = norm_back(
        inputs, inverse_rms(inputs), gain_ref[...].reshape(1, -1), grad_normed
    )
    grad_tokens_ref[...] = grad_rows + attention_ref[...].astype(FULL)
    table = jnp.concatenate([table_ref[...], jnp.zeros((heads, width - buckets), FULL)], axis=1)
    early = -(-(experts + 1) // 8) * 8
    small_ref[...] = jnp.concatenate(
        [
            router_own_ref[...] + router_came_ref[...],
            ffn_ref[...],
            jnp.zeros((early - experts - 1, width), FULL),
            grad_gain,
            table,
            jnp.zeros((small_ref.shape[0] - early - heads - 1, width), FULL),
        ],
        axis=0,
    ).astype(small_ref.dtype)


def line_chunks(totals, refs, total_refs, shared=()):
    mine = lax.rem(lax.axis_index("expert") // PLANE, LINE)
    for total, total_ref in zip(totals, total_refs):
        total_ref[...] = total
    for other, ref in enumerate(refs):
        chunks = []
        for total_ref in total_refs:
            rows = total_ref.shape[0] // LINE
            at = pl.multiple_of((mine ^ other) * rows, 8)
            chunks.append(total_ref[pl.ds(at, rows), :])
        ref[...] = jnp.concatenate(chunks + list(shared), axis=0).astype(ref.dtype)
        ref.send()


def sums_kernel(*refs):
    parts, nears, fars, normed_ref, small_ref = refs[0:4], refs[4:7], refs[7:10], *refs[10:12]
    outs, total_refs = refs[12:16], refs[16:20]
    own_rows = normed_ref.shape[0] // 2
    rows = total_refs[0].shape[0]
    pieces = normed_ref.shape[1] // parts[0].shape[1]
    output = 0.0
    weights = 0.0
    for at, part in enumerate(parts):
        output = output + jnp.concatenate(
            [part[(3 + piece) * rows : (4 + piece) * rows, :] for piece in range(pieces)], axis=1
        ).astype(FULL)
        near = nears[at - 1][...] if at else normed_ref[0:own_rows]
        far = fars[at - 1][...] if at else normed_ref[own_rows:]
        weights = weights + product(part[0 : 3 * rows, 0:own_rows], near)
        weights = weights + product(part[0 : 3 * rows, own_rows:], far)
    totals = (weights[0:rows], weights[rows : 2 * rows], weights[2 * rows :], output)
    line_chunks(totals, outs, total_refs, (small_ref[...].astype(FULL),))


def summed(refs, rows=slice(None)):
    near = refs[0][rows, :].astype(FULL) + refs[1][rows, :].astype(FULL)
    far = refs[2][rows, :].astype(FULL) + refs[3][rows, :].astype(FULL)
    return near + far


def line_sum_kernel(*refs):
    total = summed(refs[0:LINE])
    for out_ref in refs[LINE:]:
        out_ref[...] = total[0 : out_ref.shape[0]].astype(out_ref.dtype)


def assemble_kernel(*refs):
    chunk_refs = refs[0 : PLANE * LINE]
    value_ref, query_ref, key_ref, output_ref, router_ref, ffn_ref, attn_ref, table_ref = refs[
        PLANE * LINE : -3
    ]
    totals = refs[-3:] + (output_ref.ref,)
    member = lax.rem(lax.axis_index("expert"), PLANE)
    floor = lax.rem(lax.axis_index("expert") // PLANE, LINE)
    rows = output_ref.shape[0] // PLANE // LINE
    for along in range(LINE):
        for across in range(PLANE):
            chunk = chunk_refs[along * PLANE + across][0 : 4 * rows, :].astype(FULL)
            at = pl.multiple_of(((member ^ across) * LINE + (floor ^ along)) * rows, 8)
            for weight, total_ref in enumerate(totals):
                total_ref[pl.ds(at, rows), :] = chunk[weight * rows : (weight + 1) * rows]
    output_ref.send()
    for total_ref, ref in zip(totals, (value_ref, query_ref, key_ref)):
        ref[...] = total_ref[...].T
        ref.send()
    small = summed(chunk_refs[0:PLANE], slice(4 * rows, None))
    experts = router_ref.shape[0]
    heads, buckets = table_ref.shape
    late = -(-(experts + 1) // 8) * 8
    router_ref[...] = small[0:experts]
    ffn_ref[...] = small[experts : experts + 1].reshape(-1)
    attn_ref[...] = small[late : late + 1].reshape(-1)
    table_ref[...] = small[late + 1 : late + 1 + heads, 0:buckets]


def expert_grads_kernel(
    rows_ref,
    rows_far_ref,
    grad_produced_ref,
    grad_produced_far_ref,
    active_ref,
    active_far_ref,
    grad_pre_ref,
    grad_pre_far_ref,
    grad_in_ref,
    grad_out_ref,
    done_ref,
):
    done_ref[...] = jnp.zeros_like(done_ref)
    grad_in_ref[...] = product(rows_ref[...], grad_pre_ref[...], 0, 0) + product(
        rows_far_ref[...], grad_pre_far_ref[...], 0, 0
    )
    grad_out_ref[...] = product(active_ref[...], grad_produced_ref[...], 0, 0) + product(
        active_far_ref[...], grad_produced_far_ref[...], 0, 0
    )


def expert_grads(rows, rows_far, grad_produced, grad_produced_far, *wide):
    slots, width = rows.shape
    units = wide[0].shape[1]
    block = 768
    fixed = pl.BlockSpec((slots, width), lambda step: (0, 0))
    moving = pl.BlockSpec((slots, block), lambda step: (0, step))
    return pl.pallas_call(
        expert_grads_kernel,
        grid=(units // block,),
        out_shape=[
            jax.ShapeDtypeStruct((width, units), FULL),
            jax.ShapeDtypeStruct((units, width), FULL),
            jax.ShapeDtypeStruct((8, 128), FULL),
        ],
        in_specs=[fixed] * 4 + [moving] * 4,
        out_specs=[
            pl.BlockSpec((width, block), lambda step: (0, step)),
            pl.BlockSpec((block, width), lambda step: (step, 0)),
            pl.BlockSpec((8, 128), lambda step: (0, 0)),
        ],
        compiler_params=pltpu.CompilerParams(vmem_limit_bytes=56 * MEGABYTE),
        cost_estimate=pl.CostEstimate(flops=0, bytes_accessed=0, transcendentals=0),
    )(rows, rows_far, grad_produced, grad_produced_far, *wide)


def block_out_kernel(place_ref, returned_ref, hidden_ref, out_ref):
    out_ref[...] = (
        hidden_ref[...] + product(place_ref[...], returned_ref[...], 0, 0)
    ).astype(LOW)


def shards(
    tokens,
    attn_gain,
    query_weight,
    key_weight,
    value_weight,
    output_weight,
    bias_table,
    ffn_gain,
    router_weight,
    expert_in,
    expert_out,
    routes,
    lengths,
    cotangent,
):
    group_rows, width = tokens.shape
    own_rows = cotangent.shape[0]
    heads = bias_table.shape[1]
    buckets = bias_table.shape[0]
    columns = query_weight.shape[1]
    head_size = columns // heads
    sources = lax.axis_size("expert")
    experts = router_weight.shape[1]
    capacity = 2 * own_rows // experts
    slots = experts * capacity
    beyond = sources // (PLANE * LINE)
    router_rows = router_weight.T

    def swap(item):
        return lax.ppermute(item, "shard", [(0, 1), (1, 0)])

    def hop(item, distance):
        return lax.ppermute(item, "expert", [(at, at ^ distance) for at in range(sources)])

    def around(items, stride):
        return tuple(hop(item, stride * (step + 1)) for step, item in enumerate(items))

    def exchange(rows):
        parts = rows.reshape(sources, slots // sources, rows.shape[1])
        came = lax.all_to_all(parts, "expert", split_axis=0, concat_axis=0, tiled=True)
        return came.reshape(rows.shape)

    def beyond_sum(item):
        if beyond == 1:
            return item
        groups = [
            [near + PLANE * LINE * far for far in range(beyond)] for near in range(PLANE * LINE)
        ]
        return lax.psum(item, "expert", axis_index_groups=groups)

    in_own, out_own = expert_in[0], expert_out[0]
    in_came, out_came = swap(in_own), swap(out_own)
    own, other, qkv, probs, normed, mixed = run(
        functools.partial(forward_kernel, head_size=head_size),
        [
            ((own_rows, width), FULL),
            ((own_rows, width), FULL),
            ((group_rows, 3 * columns), LOW),
            ((heads, group_rows, group_rows), LOW),
            ((group_rows, width), LOW),
            ((group_rows, columns), LOW),
        ],
        (
            lengths,
            tokens,
            attn_gain,
            query_weight,
            key_weight,
            value_weight,
            bias_table.T,
            output_weight,
        ),
        scratch=(pltpu.VMEM((group_rows, width), FULL),),
        scalars=1,
    )
    place, hidden, sent, normed_own = run(
        functools.partial(hidden_kernel, experts=experts, capacity=capacity),
        [
            ((slots, own_rows), LOW),
            ((own_rows, width), FULL),
            ((slots, 2 * width), LOW),
            ((own_rows, width), LOW),
        ],
        (routes.reshape(1, own_rows), cotangent, tokens, own, ffn_gain, normed, swap(other)),
    )
    normed_near = around((normed_own,) * 3, 1)
    floors = LINE if beyond == 1 else 1
    (
        back,
        grad_back,
        grad_router,
        rows,
        grad_produced,
        active_own,
        active_came,
        grad_pre_own,
        grad_pre_came,
        *floor_back,
    ) = run(
        expert_kernel,
        [
            ((slots, width), LOW),
            ((slots, width), LOW),
            ((experts, width), FULL),
            ((slots, width), LOW),
            ((slots, width), LOW),
        ]
        + [((slots, in_own.shape[1]), LOW)] * 4
        + [((slots // floors, width), LOW)] * floors,
        (exchange(sent), router_rows, in_own, out_own, in_came, out_came),
        scratch=(
            pltpu.VMEM((2, *in_own.shape), LOW),
            pltpu.VMEM((2, *out_own.shape), LOW),
            pltpu.SemaphoreType.DMA((4,)),
        ),
        raw=(2, 3, 4, 5),
        after=normed_near,
    )
    returned_grads = exchange(grad_back)
    rows_far, grad_produced_far = swap(rows), swap(grad_produced)
    active_far, grad_pre_far = swap(active_came), swap(grad_pre_came)
    grad_router_came = swap(grad_router)
    place_came, hidden_came, cotangent_came = swap(place), swap(hidden), swap(cotangent)
    small_rows = -(-(experts + 1) // 8) * 8
    part_rows = columns // PLANE
    attention, grad_ffn, grads_low, grad_table, *parts = run(
        functools.partial(attention_back_kernel, head_size=head_size, bucket_total=buckets),
        [
            ((group_rows, width), LOW),
            ((1, width), FULL),
            ((group_rows, 3 * columns), LOW),
            ((heads, buckets), FULL),
        ]
        + [((part_rows * (3 + width // group_rows), group_rows), LOW)] * PLANE,
        (
            place,
            place_came,
            hidden,
            hidden_came,
            ffn_gain,
            cotangent,
            cotangent_came,
            returned_grads,
            swap(returned_grads),
            output_weight,
            mixed,
            qkv,
            probs,
        ),
        scratch=(
            pltpu.VMEM((group_rows, 3 * columns), FULL),
            pltpu.VMEM((3 * columns, group_rows), FULL),
            pltpu.VMEM((columns, width), FULL),
        ),
        after=(
            rows_far,
            grad_produced_far,
            active_far,
            grad_pre_far,
            grad_router_came,
        ),
    )
    parts = (parts[0],) + around(parts[1:], 1)
    grads_came = swap(grads_low)
    weights = (value_weight, query_weight, key_weight)
    weights_came = tuple(swap(item) for item in weights)
    normed_far = tuple(swap(item) for item in normed_near)
    late_rows = -(-(heads + 1) // 8) * 8
    grad_tokens, small = run(
        grad_tokens_kernel,
        [
            ((group_rows, width), FULL),
            ((small_rows + late_rows, width), LOW),
        ],
        (
            tokens,
            attn_gain,
            attention,
            grad_router,
            grad_router_came,
            grad_ffn,
            grad_table,
            grads_low,
            *weights,
            *weights_came,
            grads_came,
        ),
    )
    if beyond == 1:
        floor_back = (floor_back[0],) + around(floor_back[1:], PLANE)
    chunk_rows = 4 * part_rows // LINE
    all_rows = chunk_rows + small_rows + late_rows
    chunks = run(
        sums_kernel,
        [((all_rows, width), LOW)] * LINE,
        parts + normed_near + normed_far + (normed, small),
        scratch=(pltpu.VMEM((part_rows, width), FULL),) * 4,
        grant=24,
        after=tuple(floor_back[1:]),
    )
    chunks = (chunks[0],) + around(chunks[1:], PLANE)
    grad_expert_in, grad_expert_out, done = expert_grads(
        rows,
        rows_far,
        grad_produced,
        grad_produced_far,
        active_own,
        active_far,
        grad_pre_own,
        grad_pre_far,
    )
    if beyond == 1:
        back = run(
            member_rows_kernel, [((slots // PLANE, width), LOW)] * PLANE, floor_back, after=(chunks[1],)
        )
        back = (back[0],) + around(back[1:], 1)
        block_out, returned_done = run(
            returned_rows_kernel,
            [((own_rows, width), LOW), ((8, 128), FULL)],
            tuple(back) + (place, hidden),
            scratch=(pltpu.VMEM((slots, width), LOW),),
        )
    else:
        (block_out,) = run(
            block_out_kernel, [((own_rows, width), LOW)], (place, exchange(back), hidden)
        )
    if beyond == 1:
        whole, chunk = run(
            line_sum_kernel,
            [((all_rows, width), LOW), ((chunk_rows, width), LOW)],
            chunks,
            near=True,
            after=(done,),
        )
    else:
        (whole,) = run(line_sum_kernel, [((all_rows, width), FULL)], chunks)
        whole = beyond_sum(whole).astype(LOW)
        chunk = whole[0:chunk_rows]
    gathered = (whole,) + around((whole,) * 3, 1)
    opposite = gathered[PLANE - 1]
    for along, item in enumerate(around((chunk,) * 3, PLANE)):
        near_two = around((item,) * 2, 1)
        if along < 2:
            third = hop(opposite, PLANE * (along + 1))
        else:
            third = hop(item, PLANE - 1)
        gathered += (item,) + near_two + (third,)
    (
        grad_value,
        grad_query,
        grad_key,
        grad_output,
        grad_router,
        grad_ffn_gain,
        grad_attn_gain,
        grad_table,
    ) = run(
        assemble_kernel,
        [((width, columns), FULL)] * 3
        + [((columns, width), FULL), ((experts, width), FULL), ((width,), FULL), ((width,), FULL)]
        + [((heads, buckets), FULL)],
        gathered,
        scratch=(pltpu.VMEM((columns, width), FULL),) * 3,
        after=(block_out,),
    )
    grad_router = grad_router.T
    grad_table = grad_table.T
    return (
        block_out,
        grad_tokens,
        grad_attn_gain,
        grad_query,
        grad_key,
        grad_value,
        grad_output,
        grad_table,
        grad_ffn_gain,
        grad_router,
        grad_expert_in[None],
        grad_expert_out[None],
    )


def solution(mesh):
    return jax.shard_map(
        shards,
        mesh=mesh,
        in_specs=(
            P("expert", None),
            P(),
            P(None, "shard"),
            P(None, "shard"),
            P(None, "shard"),
            P("shard", None),
            P(None, "shard"),
            P(),
            P(),
            P("expert", None, "shard"),
            P("expert", "shard", None),
            P(("expert", "shard"), None),
            P("expert", None),
            P(("expert", "shard"), None),
        ),
        out_specs=(
            P(("expert", "shard"), None),
            P("expert", None),
            P(),
            P(None, "shard"),
            P(None, "shard"),
            P(None, "shard"),
            P("shard", None),
            P(None, "shard"),
            P(),
            P(),
            P("expert", None, "shard"),
            P("expert", "shard", None),
        ),
        check_vma=False,
    )
```
